128 devices in a mesh: axial: 16 (over x, y), azim: 8 (over z, core).
Axes of the slice: x: 4, y: 4, z: 4, core: 2. Of those that a mesh axis runs over, the one named last changes fastest.
Arguments:
- specific_heat_content: float32 [256, 1024, 512], P('axial', 'azim'), may hold values from -8 to 8
- phase: float32 [1024, 256, 256], P(('axial', 'azim')), may hold values from 0 to 1
- mobility: float32 [1024, 256, 256], P(('axial', 'azim')), may hold values from 0.5 to 2.4
- positions: int32 [1024, 3], replicated, may hold values from 0 to 1023, as said below
- counts: int32 [128], P(('axial', 'azim')), may hold values from 1 to 8, as said below
- neighbours: int32 [1024, 2], P(('axial', 'azim')), may hold values from 0 to 1023, as said below
Outputs:
- enthalpy_out: float32 [256, 1024, 512], P('axial', 'azim')
- phase_out: float32 [1024, 256, 256], P(('axial', 'azim'))
The draws below stay inside these ranges and needn't reach their ends.
Inputs may be any that keep to these rules, and one draw needn't show every extreme that they name: `positions`: each patch lies at a cell of the grid, along each dimension within 0 to 255, 1023 and 511. `counts`: every device holds at least one live patch in its first slots; exactly one device holds 8. `neighbours`: for a live slot both entries are live slots of devices with the same azim index; in each azim index the live slots form one closed chain along the front through all of them. A slot that is not live names itself twice.
All inputs are finite; a program needn't handle non-finite values.
Results may differ from the reference program's by a relative error of at most 0.00002.
Values sent between devices are 32-bit elements; how exact they have to be, the bound alone decides.
A program may use at most 128 MiB of HBM per device.

```python
import math
import jax
import jax.numpy as jnp

PATCH_SIDE = 256
PATCH_CAP = 8
PHASE_STEPS = 6
NX = 256
NY = 1024
NZ = 512
SLOTS = 1024
N_AZIM = 8
DEVICES = 128


def slot_layout(key):
    count_key, busy_key, order_key = jax.random.split(key, 3)
    counts = jax.random.randint(count_key, (DEVICES,), 1, max(PATCH_CAP // 2, 2))
    busiest = jax.random.randint(busy_key, (), 0, DEVICES)
    counts = jnp.where(jnp.arange(DEVICES) == busiest, PATCH_CAP, counts).astype(jnp.int32)
    slot_index = jnp.arange(SLOTS, dtype=jnp.int32)
    device = slot_index // PATCH_CAP
    column = device % N_AZIM
    alive = slot_index % PATCH_CAP < counts[device]
    scores = jax.random.permutation(order_key, SLOTS).astype(jnp.int32)
    sort_key = column * (2 * SLOTS) + jnp.where(alive, 0, SLOTS) + scores
    sorted_order = jnp.argsort(sort_key).astype(jnp.int32)
    placed = jnp.argsort(sorted_order).astype(jnp.int32)
    per_column = SLOTS // N_AZIM
    column_live = jnp.sum(counts.reshape(DEVICES // N_AZIM, N_AZIM), axis=0)
    start = column * per_column
    total = column_live[column]
    rank = placed - start
    following = sorted_order[start + (rank + 1) % total]
    preceding = sorted_order[start + (rank + total - 1) % total]
    neighbours = jnp.stack([jnp.where(alive, preceding, slot_index), jnp.where(alive, following, slot_index)], axis=1)
    return (counts, neighbours.astype(jnp.int32))


def draw_counts(key, part):
    return slot_layout(key)[0]


def draw_neighbours(key, part):
    return slot_layout(key)[1]


def draw_positions(key, part):
    key = jax.random.fold_in(key, 7)
    leading_key, second_key, third_key = jax.random.split(key, 3)
    axial_cell = jax.random.randint(leading_key, (SLOTS,), 0, NX)
    azim_cell = jax.random.randint(second_key, (SLOTS,), 0, NY)
    radial_cell = jax.random.randint(third_key, (SLOTS,), 0, NZ)
    return jnp.stack([axial_cell, azim_cell, radial_cell], axis=1).astype(jnp.int32)


def steps_of(stream_key, extent, shards, least, high):
    loudness, own = 1.0, jax.random.fold_in(stream_key, 6)
    for position, parts in shards:
        steps = jnp.exp(jax.random.uniform(jax.random.fold_in(own, position), (parts,), jnp.float32, least / len(shards), high / len(shards)))
        loudness = loudness * jnp.repeat(steps, extent[position] // parts).reshape([-1 if axis == position else 1 for axis in range(len(extent))])
    return loudness


def bell_draw(own_key, extent, width, limit, pieces=(), kind=jnp.bfloat16):
    drawn = width * jax.random.normal(own_key, extent, jnp.float32)
    if pieces:
        drawn = drawn * steps_of(own_key, extent, pieces, -0.22, 0.18)
    return jnp.clip(drawn, -limit, limit).astype(kind)


def setup_inputs(seed: int = 0) -> dict:
    key_of = jax.random.split(jax.random.key(seed), 7)
    return {
        "specific_heat_content": bell_draw(key_of[0], (NX, NY, NZ), 1.5, 8.0, ((0, 16), (1, 8)), jnp.float32),
        "phase": jnp.clip(1.0 * jax.random.uniform(key_of[1], (SLOTS, PATCH_SIDE, PATCH_SIDE), jnp.float32) ** steps_of(key_of[1], (SLOTS, PATCH_SIDE, PATCH_SIDE), ((0, 128),), -0.2, 0.2), 0.0, 1.0),
        "mobility": jnp.clip(jnp.exp(math.log(2.4) - 1.56861596 * jax.random.uniform(key_of[2], (SLOTS, PATCH_SIDE, PATCH_SIDE), jnp.float32) ** steps_of(key_of[2], (SLOTS, PATCH_SIDE, PATCH_SIDE), ((0, 128),), -0.2, 0.2)), 0.5, 2.4),
        "positions": draw_positions(jax.random.fold_in(key_of[6], 71), 0),
        "counts": draw_counts(jax.random.fold_in(key_of[6], 71), 0),
        "neighbours": draw_neighbours(jax.random.fold_in(key_of[6], 71), 0),
    }


DT_MACRO = 0.1
DT_PHASE = 0.1
LATENT_HEAT = 1.0
DRIVE_GAIN = 2.0
COUPLING = 20.0


def thermal_distribution(quantity_lines):
    return jnp.minimum(quantity_lines, 0.0) + jnp.maximum(quantity_lines - LATENT_HEAT, 0.0)


def advance(current, mobility, drive, column_pad):
    solid_row = jnp.ones_like(current[:, :1, :])
    liquid_row = jnp.zeros_like(current[:, :1, :])
    row_pad = jnp.concatenate([solid_row, current, liquid_row], axis=1)
    diffusion_operator = row_pad[:, :-2] + row_pad[:, 2:] + column_pad[:, :, :-2] + column_pad[:, :, 2:] - 4.0 * current
    reaction = current * (1.0 - current) * (current - 0.5 - DRIVE_GAIN * drive)
    return current + DT_PHASE * mobility * (diffusion_operator + reaction)


def reference(specific_heat_content, phase, mobility, positions, counts, neighbours):
    thermal_lines = thermal_distribution(specific_heat_content)
    lengthwise_margin = jnp.pad(thermal_lines, ((1, 1), (0, 0), (0, 0)))
    angular_margin = jnp.pad(thermal_lines, ((0, 0), (1, 1), (0, 0)), mode="wrap")
    spoke_margin = jnp.pad(thermal_lines, ((0, 0), (0, 0), (1, 1)))
    diffusion_operator = lengthwise_margin[2:] + lengthwise_margin[:-2] + angular_margin[:, 2:] + angular_margin[:, :-2] + spoke_margin[:, :, 2:] + spoke_margin[:, :, :-2] - 6.0 * thermal_lines
    warmed_snapshot = specific_heat_content + DT_MACRO * diffusion_operator
    chilled_snapshot = thermal_distribution(warmed_snapshot)
    patch_temps = chilled_snapshot[positions[:, 0], positions[:, 1], positions[:, 2]]
    slot_index = jnp.arange(SLOTS, dtype=jnp.int32)
    live_slots = (slot_index % PATCH_CAP) < counts[slot_index // PATCH_CAP]
    drive = patch_temps[:, None, None]
    current = phase
    for iteration in range(PHASE_STEPS):
        left = current[:, :, -1][neighbours[:, 0]]
        right = current[:, :, 0][neighbours[:, 1]]
        column_pad = jnp.concatenate([left[:, :, None], current, right[:, :, None]], axis=2)
        current = advance(current, mobility, drive, column_pad)
    latent = jnp.where(live_slots, COUPLING * jnp.mean(current - phase, axis=(1, 2)), 0.0)
    phase_out = jnp.where(live_slots[:, None, None], current, phase)
    enthalpy_out = warmed_snapshot.at[positions[:, 0], positions[:, 1], positions[:, 2]].add(latent)
    return enthalpy_out, phase_out
```

```python
import jax
import jax.numpy as jnp
from jax import lax
from jax.experimental import pallas as pl
from jax.experimental.pallas import tpu as pltpu
from jax.sharding import PartitionSpec as P

PHASE_STEPS = 6
DT_MACRO = 0.1
DT_PHASE = 0.1
LATENT_HEAT = 1.0
DRIVE_GAIN = 2.0
COUPLING = 20.0

NA = 16
NB = 8
SLOTS = 8
SIDE = 256
CX, CY, CZ = 16, 128, 512
CAP = 6
EDGE_ROWS = 24
MESH = pl.DeviceIdType.MESH
F32 = jnp.float32
I32 = jnp.int32
VMEM = pltpu.VMEM
SMEM = pltpu.SMEM
DMA = pltpu.SemaphoreType.DMA


def extended(value, sides, width, wrap):
    for axis, dim in sides:
        size, length = (lax.axis_size(axis), value.shape[dim])
        up = [(i, (i + 1) % size) for i in range(size if wrap else size - 1)]
        down = [(j, i) for i, j in up]
        last = lax.slice_in_dim(value, length - width, length, axis=dim)
        initial = lax.slice_in_dim(value, 0, width, axis=dim)
        before = lax.ppermute(last, axis, up)
        after = lax.ppermute(initial, axis, down)
        value = jnp.concatenate([before, value, after], axis=dim)
    return value


def thermal_distribution(quantity_lines):
    return jnp.minimum(quantity_lines, 0.0) + jnp.maximum(quantity_lines - LATENT_HEAT, 0.0)


def advance(current, mobility, drive, column_pad):
    solid_row = jnp.ones_like(current[:, :1, :])
    liquid_row = jnp.zeros_like(current[:, :1, :])
    row_pad = jnp.concatenate([solid_row, current, liquid_row], axis=1)
    diffusion_operator = (
        row_pad[:, :-2]
        + row_pad[:, 2:]
        + column_pad[:, :, :-2]
        + column_pad[:, :, 2:]
        - 4.0 * current
    )
    reaction = current * (1.0 - current) * (current - 0.5 - DRIVE_GAIN * drive)
    return current + DT_PHASE * mobility * (diffusion_operator + reaction)


def general(specific_heat_content, phase, mobility, positions, counts, neighbours):
    thermal_lines = thermal_distribution(specific_heat_content)
    lengthwise_margin = extended(thermal_lines, (("axial", 0),), 1, False)
    angular_margin = extended(thermal_lines, (("azim", 1),), 1, True)
    spoke_margin = jnp.pad(thermal_lines, ((0, 0), (0, 0), (1, 1)))
    diffusion_operator = (
        lengthwise_margin[2:]
        + lengthwise_margin[:-2]
        + angular_margin[:, 2:]
        + angular_margin[:, :-2]
        + spoke_margin[:, :, 2:]
        + spoke_margin[:, :, :-2]
        - 6.0 * thermal_lines
    )
    warmed_snapshot = specific_heat_content + DT_MACRO * diffusion_operator
    chilled_snapshot = thermal_distribution(warmed_snapshot)
    cells_x, cells_y, cells_z = specific_heat_content.shape
    local_x = positions[:, 0] - lax.axis_index("axial") * cells_x
    local_y = positions[:, 1] - lax.axis_index("azim") * cells_y
    inside = (local_x >= 0) & (local_x < cells_x) & (local_y >= 0) & (local_y < cells_y)
    flat_index = (
        jnp.clip(local_x, 0, cells_x - 1) * (cells_y * cells_z)
        + jnp.clip(local_y, 0, cells_y - 1) * cells_z
        + positions[:, 2]
    )
    sampled = jnp.where(inside, chilled_snapshot.reshape(-1)[flat_index], 0.0)
    patch_temps = lax.psum_scatter(sampled, ("axial", "azim"), scatter_dimension=0, tiled=True)
    capacity = phase.shape[0]
    live_slots = jnp.arange(capacity, dtype=jnp.int32) < counts[0]
    azim_count = lax.axis_size("azim")
    prev_rows = neighbours[:, 0] // capacity // azim_count * capacity + neighbours[:, 0] % capacity
    next_rows = neighbours[:, 1] // capacity // azim_count * capacity + neighbours[:, 1] % capacity
    drive = patch_temps[:, None, None]
    current = phase
    for iteration in range(PHASE_STEPS):
        edges = jnp.stack([current[:, :, 0], current[:, :, -1]], axis=1)
        gathered = lax.all_gather(edges, "axial", axis=0, tiled=True)
        left_edge = gathered[prev_rows, 1]
        right_edge = gathered[next_rows, 0]
        column_pad = jnp.concatenate(
            [left_edge[:, :, None], current, right_edge[:, :, None]], axis=2
        )
        current = advance(current, mobility, drive, column_pad)
    latent = jnp.where(live_slots, COUPLING * jnp.mean(current - phase, axis=(1, 2)), 0.0)
    phase_out = jnp.where(live_slots[:, None, None], current, phase)
    all_latent = lax.all_gather(latent, ("axial", "azim"), axis=0, tiled=True)
    released = jnp.where(inside, all_latent, 0.0)
    enthalpy_out = (
        warmed_snapshot.reshape(-1)
        .at[flat_index]
        .add(released)
        .reshape(specific_heat_content.shape)
    )
    return (enthalpy_out, phase_out)


def local_cell(x, y, a, b):
    return x - a * CX, ((y - b * CY + 1) & (NB * CY - 1)) - 1


def sample_kernel(pos_ref, spos_ref, e_hbm, c_ref, hits_ref, e_ref, sem):
    load = pltpu.make_async_copy(e_hbm, e_ref, sem)
    load.start()
    a, b = lax.axis_index("axial"), lax.axis_index("azim")
    lx, ly = local_cell(pos_ref[0], pos_ref[1], a, b)
    inx = (lx >= 0) & (lx < CX)
    iny = (ly >= 0) & (ly < CY)
    touched = (inx & (ly <= CY)) | (iny & (lx >= -1) & (lx <= CX))
    mark = jnp.where(touched, 1.0, 0.0).astype(F32)
    row = lax.broadcasted_iota(I32, (128, 128), 0)
    col = lax.broadcasted_iota(I32, (128, 128), 1)
    before = jnp.where(row < col, 1.0, 0.0).astype(F32)
    within = jnp.dot(mark, before, preferred_element_type=F32)
    totals = jnp.dot(mark, jnp.ones((128, 128), F32), preferred_element_type=F32)
    row8 = lax.broadcasted_iota(I32, (8, 8), 0)
    col8 = lax.broadcasted_iota(I32, (8, 8), 1)
    above = jnp.dot(jnp.where(col8 < row8, 1.0, 0.0).astype(F32), totals, preferred_element_type=F32)
    rank = jnp.where(touched, within + above, -1.0)
    linear = lax.broadcasted_iota(I32, (8, 128), 0) * 128 + lax.broadcasted_iota(I32, (8, 128), 1)
    count = jnp.sum(mark).astype(I32)
    hits_ref[0] = count
    c_ref[...] = jnp.zeros((8, 128), F32)
    lane = lax.broadcasted_iota(I32, (1, CZ), 1)
    load.wait()
    group = 4

    def chunk(i, carry):
        acc = c_ref[...]
        for j in range(group):
            h = i * group + j
            s = jnp.sum(jnp.where(rank == h.astype(F32), linear, 0))
            hits_ref[h + 1] = s
            valid = h < count
            px, py = local_cell(spos_ref[s], spos_ref[NA * NB * SLOTS + s], a, b)
            z = spos_ref[2 * NA * NB * SLOTS + s]
            okx = (px >= 0) & (px < CX) & valid
            oky = (py >= 0) & (py < CY) & valid
            x0 = jnp.clip(px, 0, CX - 1)
            y0 = jnp.clip(py, 0, CY - 1)

            def part(x, y, ok):
                t = thermal_distribution(e_ref[jnp.clip(x, 0, CX - 1), pl.ds(jnp.clip(y, 0, CY - 1), 1), :])
                return jnp.where(ok, t, 0.0)

            inside = okx & oky
            own = jnp.where(inside, e_ref[x0, pl.ds(y0, 1), :], 0.0)
            t = thermal_distribution(own)
            ring = (
                part(px - 1, y0, oky & (px >= 1) & (px <= CX))
                + part(px + 1, y0, oky & (px >= -1) & (px < CX - 1))
                + part(x0, py - 1, okx & (py >= 1) & (py <= CY))
                + part(x0, py + 1, okx & (py >= -1) & (py < CY - 1))
            )
            here = lane == z
            beside = (lane == z - 1) | (lane == z + 1)
            value = jnp.where(here, own + DT_MACRO * (ring - 6.0 * t), 0.0) + jnp.where(beside, DT_MACRO * t, 0.0)
            acc = acc + jnp.where((linear == s) & valid, jnp.sum(value, keepdims=True), 0.0)
        c_ref[...] = acc
        return carry

    lax.fori_loop(0, (count + group - 1) // group, chunk, 0)


def lane_sum(halves, lane):
    first, second = halves
    l0, l1 = pltpu.roll(first, 1, 1), pltpu.roll(second, 1, 1)
    r0, r1 = pltpu.roll(first, 127, 1), pltpu.roll(second, 127, 1)
    low, high = lane == 0, lane == 127
    return (
        jnp.where(low, 1.0, l0) + jnp.where(high, r1, r0),
        jnp.where(low, l0, l1) + jnp.where(high, 0.0, r1),
    )


def phase_step(halves, rates, k1, k4, lane):
    rows = halves[0].shape[0]
    beside = lane_sum(halves, lane)
    out = []
    for h in range(2):
        c = halves[h]
        around = beside[h] + (pltpu.roll(c, 1, 0) + pltpu.roll(c, rows - 1, 0))
        out.append(c + rates[h] * (around + c * (c * (k1 - c) - k4)))
    return tuple(out)


def main_kernel(
    send_ref, recv_ref, place_ref, c_ref, flag_ref, live_ref, e_hbm, phase_hbm, mob_hbm,
    heated_ref, out_ref, latent_ref, over_ref,
    e_ref, t_ref, p_ref, m_ref, pt, mt, ct, eb, sb, rb, stp, stm,
    hx, hy, ty, c_out, c1, c2, sum1, lat, l1, l2, latsum, nb_t,
    load_sem, s1s, s1r, s2s, s2r, es, er, hxs, hxr, hys, hyr, l1s, l1r, l2s, l2r,
):
    a, b = lax.axis_index("axial"), lax.axis_index("azim")
    ax = [(lax.rem(a + i, NA), b) for i in range(1, NA)]
    az = [(a, lax.rem(b + i, NB)) for i in range(1, NB)]
    barrier = pltpu.get_barrier_semaphore()
    for peer in az + ax:
        pl.semaphore_signal(barrier, inc=1, device_id=peer, device_id_type=MESH)

    load_p = pltpu.make_async_copy(phase_hbm, p_ref, load_sem.at[0])
    load_m = pltpu.make_async_copy(mob_hbm, m_ref, load_sem.at[1])
    load_e = pltpu.make_async_copy(e_hbm, e_ref, load_sem.at[2])
    load_p.start()
    load_m.start()
    load_e.start()
    for j in range(NB):
        c_out[j, 0:1, :] = c_ref[j : j + 1, :]
        c_out[j, 1:2, :] = flag_ref[...]
    load_p.wait()
    load_m.wait()

    @pl.loop(0, SLOTS)
    def _(s):
        p = p_ref[s].T
        m = m_ref[s].T * DT_PHASE
        for h in range(2):
            ph, mh = p[:, h * 128 : h * 128 + 128], m[:, h * 128 : h * 128 + 128]
            pt[s, h] = ph
            mt[s, h] = mh
            base = h * 12
            eb[2 * s, base : base + 6] = ph[0:6]
            eb[2 * s, base + 6 : base + 11] = mh[0:5]
            eb[2 * s + 1, base : base + 6] = ph[250:256]
            eb[2 * s + 1, base + 6 : base + 11] = mh[251:256]
            eb[2 * s, base + 11 : base + 12] = jnp.zeros((1, 128), F32)
            eb[2 * s + 1, base + 11 : base + 12] = jnp.zeros((1, 128), F32)

    pl.semaphore_wait(barrier, len(az) + len(ax))

    for i, peer in enumerate(az):
        pltpu.make_async_remote_copy(
            c_out.at[peer[1]], c1.at[b], s1s, s1r, device_id=peer, device_id_type=MESH
        ).start()
    c1[b] = c_out[b]

    @pl.loop(0, (NA - 1) * CAP)
    def _(n):
        sb[n] = eb[send_ref[n]]

    for i, peer in enumerate(ax):
        pltpu.make_async_remote_copy(
            sb.at[pl.ds(i * CAP, CAP)], rb.at[pl.ds(i * CAP, CAP)], es, er, device_id=peer, device_id_type=MESH
        ).start()

    load_e.wait()

    @pl.loop(0, CX)
    def _(x):
        t = thermal_distribution(e_ref[x])
        t_ref[x] = t
        ty[0, x] = t[0:1]
        ty[1, x] = t[CY - 1 : CY]

    up_b, down_b = (a, lax.rem(b + 1, NB)), (a, lax.rem(b + NB - 1, NB))
    up_a, down_a = (lax.rem(a + 1, NA), b), (lax.rem(a + NA - 1, NA), b)
    y_up = pltpu.make_async_remote_copy(ty.at[1], hy.at[0], hys.at[0], hyr.at[0], device_id=up_b, device_id_type=MESH)
    y_down = pltpu.make_async_remote_copy(ty.at[0], hy.at[1], hys.at[1], hyr.at[1], device_id=down_b, device_id_type=MESH)
    y_up.start()
    y_down.start()

    whole1 = pltpu.make_async_remote_copy(
        c_out.at[pl.ds(0, NB - 1)], c1.at[pl.ds(0, NB - 1)], s1s, s1r, device_id=az[0], device_id_type=MESH
    )
    whole1.wait_recv()
    sum1[...] = jnp.sum(c1[...], axis=0)
    for i, peer in enumerate(ax):
        pltpu.make_async_remote_copy(sum1, c2.at[a], s2s, s2r, device_id=peer, device_id_type=MESH).start()
    c2[a] = sum1[...]

    x_up = pltpu.make_async_remote_copy(
        t_ref.at[CX - 1], hx.at[0], hxs.at[0], hxr.at[0], device_id=up_a, device_id_type=MESH
    )
    x_down = pltpu.make_async_remote_copy(
        t_ref.at[0], hx.at[1], hxs.at[1], hxr.at[1], device_id=down_a, device_id_type=MESH
    )
    x_up.start()
    x_down.start()

    y_up.wait()
    y_down.wait()

    line = lax.broadcasted_iota(I32, (CY, CZ), 0)
    radial = lax.broadcasted_iota(I32, (CY, CZ), 1)

    def plane(x, below, above):
        t = t_ref[x]
        ym = jnp.where(line == 0, hy[0, x], pltpu.roll(t, 1, 0))
        yp = jnp.where(line == CY - 1, hy[1, x], pltpu.roll(t, CY - 1, 0))
        zm = jnp.where(radial == 0, 0.0, pltpu.roll(t, 1, 1))
        zp = jnp.where(radial == CZ - 1, 0.0, pltpu.roll(t, CZ - 1, 1))
        heated_ref[x] = e_ref[x] + DT_MACRO * ((below + above) + (ym + yp) + (zm + zp) - 6.0 * t)

    @pl.loop(1, CX - 1)
    def _(x):
        plane(x, t_ref[x - 1], t_ref[x + 1])

    whole2 = pltpu.make_async_remote_copy(
        c2.at[pl.ds(0, NA - 1)], c2.at[pl.ds(0, NA - 1)], s2s, s2r, device_id=ax[0], device_id_type=MESH
    )
    whole2.wait_recv()
    total = jnp.sum(c2[...], axis=0)
    over_ref[...] = total[1:2]
    temps = thermal_distribution(total[0:1])
    lanes1 = lax.broadcasted_iota(I32, (1, 128), 1)

    def temp_of(index):
        return jnp.sum(jnp.where(lanes1 == index, temps, 0.0), axis=1, keepdims=True)

    lane_full = lax.broadcasted_iota(I32, (SIDE, 128), 1)
    row_full = lax.broadcasted_iota(I32, (SIDE, 128), 0)
    body = (row_full >= 6) & (row_full < SIDE - 6)

    @pl.loop(0, SLOTS)
    def _(s):
        tau = temp_of(a * SLOTS + s)
        nb_t[s] = jnp.broadcast_to(tau, (1, 128))
        k1, k4 = 1.5 + DRIVE_GAIN * tau, 4.5 + DRIVE_GAIN * tau
        cur = (pt[s, 0], pt[s, 1])
        for _step in range(PHASE_STEPS):
            cur = phase_step(cur, (mt[s, 0], mt[s, 1]), k1, k4, lane_full)
        ct[s, 0] = cur[0]
        ct[s, 1] = cur[1]
        change = (cur[0] - pt[s, 0]) + (cur[1] - pt[s, 1])
        latsum[s] = jnp.sum(jnp.where(body, change, 0.0), axis=0, keepdims=True)

    whole_e = pltpu.make_async_remote_copy(sb, rb, es, er, device_id=ax[0], device_id_type=MESH)
    whole_e.wait_recv()
    lane_strip = lax.broadcasted_iota(I32, (24, 128), 1)
    row_strip = lax.broadcasted_iota(I32, (24, 128), 0)
    lat[...] = jnp.zeros((1, 128), F32)

    @pl.loop(0, SLOTS)
    def _(s):
        tau = nb_t[s]
        curs, rates, ks = [], [], []
        for side in range(2):
            e = 2 * s + side
            own_edge = place_ref[3 * e + 1]
            near = eb[own_edge]
            far = rb[recv_ref[e]]
            is_far = jnp.broadcast_to(place_ref[3 * e + 2], (EDGE_ROWS, 128)) > 0
            edge = jnp.where(is_far, far, near)
            other = temp_of(place_ref[3 * e])
            for h in range(2):
                ph, mh = edge[h * 12 : h * 12 + 6], edge[h * 12 + 6 : h * 12 + 11]
                if side == 0:
                    stp[side, h, 0:2] = jnp.zeros((2, 128), F32)
                    stp[side, h, 2:8] = ph
                    stp[side, h, 8:24] = pt[s, h, 0:16]
                    stm[side, h, 0:3] = jnp.zeros((3, 128), F32)
                    stm[side, h, 3:8] = mh
                    stm[side, h, 8:24] = mt[s, h, 0:16]
                else:
                    stp[side, h, 0:16] = pt[s, h, SIDE - 16 : SIDE]
                    stp[side, h, 16:22] = ph
                    stp[side, h, 22:24] = jnp.zeros((2, 128), F32)
                    stm[side, h, 0:16] = mt[s, h, SIDE - 16 : SIDE]
                    stm[side, h, 16:21] = mh
                    stm[side, h, 21:24] = jnp.zeros((3, 128), F32)
            outer = row_strip < 8 if side == 0 else row_strip >= 16
            ks.append(DRIVE_GAIN * jnp.where(outer, other, tau))
            curs.append((stp[side, 0], stp[side, 1]))
            rates.append((stm[side, 0], stm[side, 1]))
        starts = curs
        for _step in range(PHASE_STEPS):
            curs = [
                phase_step(curs[side], rates[side], 1.5 + ks[side], 4.5 + ks[side], lane_strip) for side in range(2)
            ]
        total_s = latsum[s]
        for side in range(2):
            low = 8 if side == 0 else 10
            first = 0 if side == 0 else SIDE - 6
            for h in range(2):
                ct[s, h, first : first + 6] = curs[side][h][low : low + 6]
            kept = (row_strip >= low) & (row_strip < low + 6)
            change = (curs[side][0] - starts[side][0]) + (curs[side][1] - starts[side][1])
            total_s = total_s + jnp.sum(jnp.where(kept, change, 0.0), axis=0, keepdims=True)
        value = jnp.sum(total_s, axis=1, keepdims=True) * (COUPLING / (SIDE * SIDE))
        lat[...] = jnp.where(lanes1 == a * SLOTS + s, jnp.where(live_ref[...] > 0.5, value, 0.0), lat[...])

    for i, peer in enumerate(ax):
        pltpu.make_async_remote_copy(lat, l1.at[a], l1s, l1r, device_id=peer, device_id_type=MESH).start()
    l1[a] = lat[...]

    x_up.wait()
    x_down.wait()
    plane(0, jnp.where(a > 0, 1.0, 0.0).astype(F32) * hx[0], t_ref[1])
    plane(CX - 1, t_ref[CX - 2], jnp.where(a < NA - 1, 1.0, 0.0).astype(F32) * hx[1])

    whole_l1 = pltpu.make_async_remote_copy(
        l1.at[pl.ds(0, NA - 1)], l1.at[pl.ds(0, NA - 1)], l1s, l1r, device_id=ax[0], device_id_type=MESH
    )
    whole_l1.wait_recv()
    column = jnp.sum(l1[...], axis=0)
    l2[b] = column
    for i, peer in enumerate(az):
        pltpu.make_async_remote_copy(l2.at[b], l2.at[b], l2s, l2r, device_id=peer, device_id_type=MESH).start()

    @pl.loop(0, SLOTS)
    def _(s):
        alive = jnp.sum(jnp.where(lanes1 == a * SLOTS + s, live_ref[...], 0.0), axis=1, keepdims=True)
        for h in range(2):
            final = jnp.where(alive > 0.5, ct[s, h], pt[s, h])
            out_ref[s, h * 128 : h * 128 + 128, :] = final.T

    whole_l2 = pltpu.make_async_remote_copy(
        l2.at[pl.ds(0, NB - 1)], l2.at[pl.ds(0, NB - 1)], l2s, l2r, device_id=az[0], device_id_type=MESH
    )
    whole_l2.wait_recv()
    for j in range(NB):
        latent_ref[j : j + 1, :] = l2[j]

    whole1.wait_send()
    whole2.wait_send()
    whole_e.wait_send()
    whole_l1.wait_send()
    whole_l2.wait_send()


def release_kernel(hits_ref, spos_ref, lat_ref, heated_hbm, phase_hbm, out_hbm, phase_out_hbm, grid_ref, sem):
    move = pltpu.make_async_copy(phase_hbm, phase_out_hbm, sem.at[0])
    move.start()
    load = pltpu.make_async_copy(heated_hbm, grid_ref, sem.at[1])
    load.start()
    a, b = lax.axis_index("axial"), lax.axis_index("azim")
    lane = lax.broadcasted_iota(I32, (1, CZ), 1)
    load.wait()

    def add(h, carry):
        s = hits_ref[h + 1]
        px, py = local_cell(spos_ref[s], spos_ref[NA * NB * SLOTS + s], a, b)
        z = spos_ref[2 * NA * NB * SLOTS + s]
        inside = (px >= 0) & (px < CX) & (py >= 0) & (py < CY)
        x0 = jnp.clip(px, 0, CX - 1)
        y0 = jnp.clip(py, 0, CY - 1)
        value = jnp.where(inside, lat_ref[s], 0.0)
        grid_ref[x0, pl.ds(y0, 1), :] = grid_ref[x0, pl.ds(y0, 1), :] + jnp.where(lane == z, value, 0.0)
        return carry

    lax.fori_loop(0, hits_ref[0], add, 0)
    store = pltpu.make_async_copy(grid_ref, out_hbm, sem.at[2])
    store.start()
    store.wait()
    move.wait()


def spec(space):
    return pl.BlockSpec(memory_space=space)


def seam_tables(neighbours):
    a = lax.axis_index("axial")
    column = neighbours // SLOTS // NB
    slot = neighbours % SLOTS
    halo = jnp.arange(2 * SLOTS, dtype=I32)
    source = column.reshape(-1)
    edge_there = (2 * slot + jnp.array([1, 0], I32)).reshape(-1)
    lower = halo[None, :] < halo[:, None]
    rank = jnp.sum(((source[None, :] == source[:, None]) & lower).astype(I32), axis=1)
    hop = (a - source) % NA
    far = hop > 0
    place = jnp.where(far, (hop - 1) * CAP + jnp.minimum(rank, CAP - 1), 0)
    over = jnp.max(jnp.where(far & (rank >= CAP), 1.0, 0.0))
    info = jnp.stack([source * SLOTS + slot.reshape(-1), edge_there, far.astype(I32)], axis=1).reshape(-1)
    goal = column.reshape(-1)
    key = (2 * slot + jnp.array([1, 0], I32)).reshape(-1)
    turn = jnp.sum(((goal[None, :] == goal[:, None]) & (key[None, :] < key[:, None])).astype(I32), axis=1)
    hop_out = (goal - a) % NA
    wanted = jnp.arange((NA - 1) * CAP, dtype=I32)
    chosen = ((hop_out - 1) * CAP + turn)[None, :] == wanted[:, None]
    chosen = chosen & (hop_out > 0)[None, :] & (turn < CAP)[None, :]
    sends = jnp.sum(jnp.where(chosen, halo[None, :], 0), axis=1)
    return sends.astype(I32), place.astype(I32), info.astype(I32), over


def shards(specific_heat_content, phase, mobility, positions, counts, neighbours):
    a = lax.axis_index("axial")
    pos = positions.T.reshape(3, NA, NB, SLOTS).transpose(0, 2, 1, 3).reshape(3, NB, NA * SLOTS)
    flat = pos.reshape(-1)
    sends, place, info, over = seam_tables(neighbours)
    lanes = jnp.arange(NA * SLOTS, dtype=I32)
    live = ((lanes // SLOTS == a) & (lanes % SLOTS < counts[0])).astype(F32).reshape(1, NA * SLOTS)
    flag = jnp.broadcast_to(over, (1, 128)).astype(F32)

    shares, hits = pl.pallas_call(
        sample_kernel,
        out_shape=(
            jax.ShapeDtypeStruct((NB, 128), F32),
            jax.ShapeDtypeStruct((NA * NB * SLOTS + 8,), I32),
        ),
        in_specs=[spec(VMEM), spec(SMEM), spec(pl.ANY)],
        out_specs=(spec(VMEM), spec(SMEM)),
        scratch_shapes=[VMEM((CX, CY, CZ), F32), DMA],
        compiler_params=pltpu.CompilerParams(vmem_limit_bytes=16 << 20),
        name="sample",
    )(pos, flat, specific_heat_content)

    heated, phase_new, latents, over_all = pl.pallas_call(
        main_kernel,
        out_shape=(
            jax.ShapeDtypeStruct((CX, CY, CZ), F32),
            jax.ShapeDtypeStruct((SLOTS, SIDE, SIDE), F32),
            jax.ShapeDtypeStruct((NB, 128), F32),
            jax.ShapeDtypeStruct((1, 128), F32),
        ),
        in_specs=[spec(SMEM)] * 3 + [spec(VMEM)] * 3 + [spec(pl.ANY)] * 3,
        out_specs=(spec(VMEM), spec(VMEM), spec(VMEM), spec(VMEM)),
        scratch_shapes=[
            VMEM((CX, CY, CZ), F32),
            VMEM((CX, CY, CZ), F32),
            VMEM((SLOTS, SIDE, SIDE), F32),
            VMEM((SLOTS, SIDE, SIDE), F32),
            VMEM((SLOTS, 2, SIDE, 128), F32),
            VMEM((SLOTS, 2, SIDE, 128), F32),
            VMEM((SLOTS, 2, SIDE, 128), F32),
            VMEM((2 * SLOTS, EDGE_ROWS, 128), F32),
            VMEM(((NA - 1) * CAP, EDGE_ROWS, 128), F32),
            VMEM(((NA - 1) * CAP, EDGE_ROWS, 128), F32),
            VMEM((2, 2, 24, 128), F32),
            VMEM((2, 2, 24, 128), F32),
            VMEM((2, CY, CZ), F32),
            VMEM((2, CX, 1, CZ), F32),
            VMEM((2, CX, 1, CZ), F32),
            VMEM((NB, 2, 128), F32),
            VMEM((NB, 2, 128), F32),
            VMEM((NA, 2, 128), F32),
            VMEM((2, 128), F32),
            VMEM((1, 128), F32),
            VMEM((NA, 1, 128), F32),
            VMEM((NB, 1, 128), F32),
            VMEM((SLOTS, 1, 128), F32),
            VMEM((SLOTS, 1, 128), F32),
            DMA((3,)),
            DMA, DMA, DMA, DMA, DMA, DMA,
            DMA((2,)), DMA((2,)), DMA((2,)), DMA((2,)),
            DMA, DMA, DMA, DMA,
        ],
        compiler_params=pltpu.CompilerParams(
            collective_id=0, has_side_effects=True, vmem_limit_bytes=48 << 20
        ),
        name="couple",
    )(sends, place, info, shares, flag, live, specific_heat_content, phase, mobility)

    def finish():
        return pl.pallas_call(
            release_kernel,
            out_shape=(
                jax.ShapeDtypeStruct((CX, CY, CZ), F32),
                jax.ShapeDtypeStruct((SLOTS, SIDE, SIDE), F32),
            ),
            in_specs=[spec(SMEM)] * 3 + [spec(pl.ANY)] * 2,
            out_specs=(spec(pl.ANY), spec(pl.ANY)),
            scratch_shapes=[VMEM((CX, CY, CZ), F32), DMA((3,))],
            compiler_params=pltpu.CompilerParams(vmem_limit_bytes=16 << 20),
            name="release",
        )(hits, flat, latents.reshape(-1), heated, phase_new)

    def whole():
        return general(specific_heat_content, phase, mobility, positions, counts, neighbours)

    return lax.cond(over_all[0, 0] > 0.5, whole, finish)


def solution(mesh):
    in_specs = (
        P("axial", "azim", None),
        P(("axial", "azim"), None, None),
        P(("axial", "azim"), None, None),
        P(),
        P(("axial", "azim")),
        P(("axial", "azim"), None),
    )
    out_specs = (P("axial", "azim", None), P(("axial", "azim"), None, None))
    return jax.shard_map(shards, mesh=mesh, in_specs=in_specs, out_specs=out_specs, check_vma=False)
```

```python
import jax
import jax.numpy as jnp
from jax import lax
from jax.experimental import pallas as pl
from jax.experimental.pallas import tpu as pltpu
from jax.sharding import PartitionSpec as P

PHASE_STEPS = 6
DT_MACRO = 0.1
DT_PHASE = 0.1
LATENT_HEAT = 1.0
DRIVE_GAIN = 2.0
COUPLING = 20.0

NA = 16
NB = 8
SLOTS = 8
SIDE = 256
CX, CY, CZ = 16, 128, 512
CAP = 5
HIT_CAP = 32
HIT_GROUP = 4
EDGE_ROWS = 24
MESH = pl.DeviceIdType.MESH
F32 = jnp.float32
I32 = jnp.int32
VMEM = pltpu.VMEM
SMEM = pltpu.SMEM
DMA = pltpu.SemaphoreType.DMA


def extended(value, sides, width, wrap):
    for axis, dim in sides:
        size, length = (lax.axis_size(axis), value.shape[dim])
        up = [(i, (i + 1) % size) for i in range(size if wrap else size - 1)]
        down = [(j, i) for i, j in up]
        last = lax.slice_in_dim(value, length - width, length, axis=dim)
        initial = lax.slice_in_dim(value, 0, width, axis=dim)
        before = lax.ppermute(last, axis, up)
        after = lax.ppermute(initial, axis, down)
        value = jnp.concatenate([before, value, after], axis=dim)
    return value


def thermal_distribution(quantity_lines):
    return jnp.minimum(quantity_lines, 0.0) + jnp.maximum(quantity_lines - LATENT_HEAT, 0.0)


def advance(current, mobility, drive, column_pad):
    solid_row = jnp.ones_like(current[:, :1, :])
    liquid_row = jnp.zeros_like(current[:, :1, :])
    row_pad = jnp.concatenate([solid_row, current, liquid_row], axis=1)
    diffusion_operator = (
        row_pad[:, :-2]
        + row_pad[:, 2:]
        + column_pad[:, :, :-2]
        + column_pad[:, :, 2:]
        - 4.0 * current
    )
    reaction = current * (1.0 - current) * (current - 0.5 - DRIVE_GAIN * drive)
    return current + DT_PHASE * mobility * (diffusion_operator + reaction)


def general(specific_heat_content, phase, mobility, positions, counts, neighbours):
    thermal_lines = thermal_distribution(specific_heat_content)
    lengthwise_margin = extended(thermal_lines, (("axial", 0),), 1, False)
    angular_margin = extended(thermal_lines, (("azim", 1),), 1, True)
    spoke_margin = jnp.pad(thermal_lines, ((0, 0), (0, 0), (1, 1)))
    diffusion_operator = (
        lengthwise_margin[2:]
        + lengthwise_margin[:-2]
        + angular_margin[:, 2:]
        + angular_margin[:, :-2]
        + spoke_margin[:, :, 2:]
        + spoke_margin[:, :, :-2]
        - 6.0 * thermal_lines
    )
    warmed_snapshot = specific_heat_content + DT_MACRO * diffusion_operator
    chilled_snapshot = thermal_distribution(warmed_snapshot)
    cells_x, cells_y, cells_z = specific_heat_content.shape
    local_x = positions[:, 0] - lax.axis_index("axial") * cells_x
    local_y = positions[:, 1] - lax.axis_index("azim") * cells_y
    inside = (local_x >= 0) & (local_x < cells_x) & (local_y >= 0) & (local_y < cells_y)
    flat_index = (
        jnp.clip(local_x, 0, cells_x - 1) * (cells_y * cells_z)
        + jnp.clip(local_y, 0, cells_y - 1) * cells_z
        + positions[:, 2]
    )
    sampled = jnp.where(inside, chilled_snapshot.reshape(-1)[flat_index], 0.0)
    patch_temps = lax.psum_scatter(sampled, ("axial", "azim"), scatter_dimension=0, tiled=True)
    capacity = phase.shape[0]
    live_slots = jnp.arange(capacity, dtype=jnp.int32) < counts[0]
    azim_count = lax.axis_size("azim")
    prev_rows = neighbours[:, 0] // capacity // azim_count * capacity + neighbours[:, 0] % capacity
    next_rows = neighbours[:, 1] // capacity // azim_count * capacity + neighbours[:, 1] % capacity
    drive = patch_temps[:, None, None]
    current = phase
    for iteration in range(PHASE_STEPS):
        edges = jnp.stack([current[:, :, 0], current[:, :, -1]], axis=1)
        gathered = lax.all_gather(edges, "axial", axis=0, tiled=True)
        left_edge = gathered[prev_rows, 1]
        right_edge = gathered[next_rows, 0]
        column_pad = jnp.concatenate(
            [left_edge[:, :, None], current, right_edge[:, :, None]], axis=2
        )
        current = advance(current, mobility, drive, column_pad)
    latent = jnp.where(live_slots, COUPLING * jnp.mean(current - phase, axis=(1, 2)), 0.0)
    phase_out = jnp.where(live_slots[:, None, None], current, phase)
    all_latent = lax.all_gather(latent, ("axial", "azim"), axis=0, tiled=True)
    released = jnp.where(inside, all_latent, 0.0)
    enthalpy_out = (
        warmed_snapshot.reshape(-1)
        .at[flat_index]
        .add(released)
        .reshape(specific_heat_content.shape)
    )
    return (enthalpy_out, phase_out)


def local_cell(x, y, a, b):
    return x - a * CX, ((y - b * CY + 1) & (NB * CY - 1)) - 1


def rank_hits(pos_ref, posb, a, b):
    for c in range(2):
        for r in range(8):
            posb[c, r : r + 1, :] = pos_ref[c : c + 1, r * 128 : r * 128 + 128]
    lx, ly = local_cell(posb[0], posb[1], a, b)
    inx = (lx >= 0) & (lx < CX)
    iny = (ly >= 0) & (ly < CY)
    touched = (inx & (ly <= CY)) | (iny & (lx >= -1) & (lx <= CX))
    mark = jnp.where(touched, 1.0, 0.0).astype(F32)
    row = lax.broadcasted_iota(I32, (128, 128), 0)
    col = lax.broadcasted_iota(I32, (128, 128), 1)
    before = jnp.where(row < col, 1.0, 0.0).astype(F32)
    within = jnp.dot(mark, before, preferred_element_type=F32)
    totals = jnp.dot(mark, jnp.ones((128, 128), F32), preferred_element_type=F32)
    row8 = lax.broadcasted_iota(I32, (8, 8), 0)
    col8 = lax.broadcasted_iota(I32, (8, 8), 1)
    above = jnp.dot(jnp.where(col8 < row8, 1.0, 0.0).astype(F32), totals, preferred_element_type=F32)
    rank = jnp.where(touched, within + above, -1.0)
    return rank, jnp.sum(touched.astype(I32))


def share_of(s, valid, spos_ref, e_ref, a, b, lane):
    px, py = local_cell(spos_ref[0, s], spos_ref[1, s], a, b)
    z = spos_ref[2, s]
    okx = (px >= 0) & (px < CX) & valid
    oky = (py >= 0) & (py < CY) & valid
    x0 = jnp.clip(px, 0, CX - 1)
    y0 = jnp.clip(py, 0, CY - 1)

    def part(x, y, ok):
        t = thermal_distribution(e_ref[jnp.clip(x, 0, CX - 1), pl.ds(jnp.clip(y, 0, CY - 1), 1), :])
        return jnp.where(ok, t, 0.0)

    own = jnp.where(okx & oky, e_ref[x0, pl.ds(y0, 1), :], 0.0)
    t = thermal_distribution(own)
    ring = (
        part(px - 1, y0, oky & (px >= 1) & (px <= CX))
        + part(px + 1, y0, oky & (px >= -1) & (px < CX - 1))
        + part(x0, py - 1, okx & (py >= 1) & (py <= CY))
        + part(x0, py + 1, okx & (py >= -1) & (py < CY - 1))
    )
    here = lane == z
    beside = (lane == z - 1) | (lane == z + 1)
    value = jnp.where(here, own + DT_MACRO * (ring - 6.0 * t), 0.0) + jnp.where(beside, DT_MACRO * t, 0.0)
    return jnp.sum(value, keepdims=True)


def seam_tables(nb_ref, place_ref, recv_ref, a):
    halos = range(2 * SLOTS)
    names = [nb_ref[e % 2, e // 2] for e in halos]
    source = [n // (SLOTS * NB) for n in names]
    slot = [n % SLOTS for n in names]
    over = jnp.int32(0)
    for e in halos:
        rank = jnp.int32(0)
        for f in range(e):
            rank = rank + (source[f] == source[e]).astype(I32)
        hop = (a - source[e] + NA) % NA
        far = (hop > 0).astype(I32)
        over = jnp.maximum(over, far * (rank >= CAP).astype(I32))
        recv_ref[e] = jnp.where(hop > 0, (hop - 1) * CAP + jnp.minimum(rank, CAP - 1), 0)
        place_ref[3 * e] = source[e] * SLOTS + slot[e]
        place_ref[3 * e + 1] = 2 * slot[e] + 1 - e % 2
        place_ref[3 * e + 2] = far
    key = [2 * slot[f] + 1 - f % 2 for f in halos]
    lane = lax.broadcasted_iota(I32, (1, 128), 1)
    sends = jnp.zeros((1, 128), I32)
    for f in halos:
        turn = jnp.int32(0)
        for g in halos:
            if g != f:
                turn = turn + ((source[g] == source[f]) & (key[g] < key[f])).astype(I32)
        hop = (source[f] - a + NA) % NA
        goal = jnp.where((hop > 0) & (turn < CAP), (hop - 1) * CAP + turn, -1)
        sends = sends + jnp.where(lane == goal, f, 0)
    return sends, over


def lane_sum(halves, lane):
    first, second = halves
    l0, l1 = pltpu.roll(first, 1, 1), pltpu.roll(second, 1, 1)
    r0, r1 = pltpu.roll(first, 127, 1), pltpu.roll(second, 127, 1)
    low, high = lane == 0, lane == 127
    return (
        jnp.where(low, 1.0, l0) + jnp.where(high, r1, r0),
        jnp.where(low, l0, l1) + jnp.where(high, 0.0, r1),
    )


def phase_step(halves, rates, k1, k4, lane):
    rows = halves[0].shape[0]
    beside = lane_sum(halves, lane)
    out = []
    for h in range(2):
        c = halves[h]
        around = beside[h] + (pltpu.roll(c, 1, 0) + pltpu.roll(c, rows - 1, 0))
        out.append(c + rates[h] * (around + c * (c * (k1 - c) - k4)))
    return tuple(out)


def main_kernel(
    pos_ref, spos_ref, nb_ref, count_ref, e_hbm, phase_hbm, mob_hbm,
    heated_ref, out_ref, latent_ref, over_ref, hits_ref,
    send_v, send_ref, recv_ref, place_ref, posb, shares,
    e_ref, t_ref, p_ref, m_ref, pt, mt, ct, eb, sb, rb, stp, stm,
    hx, hy, ty, c_out, c1, c2, sum1, lat, l1, l2, latsum, nb_t,
    load_sem, s1s, s1r, s2s, s2r, es, er, hxs, hxr, hys, hyr, l1s, l1r, l2s, l2r,
):
    a, b = lax.axis_index("axial"), lax.axis_index("azim")
    ax = [(lax.rem(a + i, NA), b) for i in range(1, NA)]
    az = [(a, lax.rem(b + i, NB)) for i in range(1, NB)]
    barrier = pltpu.get_barrier_semaphore()
    for peer in az + ax:
        pl.semaphore_signal(barrier, inc=1, device_id=peer, device_id_type=MESH)

    load_p = pltpu.make_async_copy(phase_hbm, p_ref, load_sem.at[0])
    load_m = pltpu.make_async_copy(mob_hbm, m_ref, load_sem.at[1])
    load_e = pltpu.make_async_copy(e_hbm, e_ref, load_sem.at[2])
    load_e.start()
    load_p.start()
    load_m.start()

    lanes1 = lax.broadcasted_iota(I32, (1, 128), 1)
    alive_all = ((lanes1 // SLOTS == a) & (lanes1 % SLOTS < count_ref[0])).astype(F32)
    sends, over = seam_tables(nb_ref, place_ref, recv_ref, a)
    send_v[...] = sends
    to_smem = pltpu.make_async_copy(send_v, send_ref, load_sem.at[3])
    to_smem.start()
    rank, count = rank_hits(pos_ref, posb, a, b)
    over = jnp.maximum(over, (count > HIT_CAP).astype(I32))
    hits_ref[0] = jnp.minimum(count, HIT_CAP)
    shares[...] = jnp.zeros((NB, 128), F32)
    linear = lax.broadcasted_iota(I32, (NB, 128), 0) * 128 + lax.broadcasted_iota(I32, (NB, 128), 1)
    lane_z = lax.broadcasted_iota(I32, (1, CZ), 1)
    load_e.wait()

    @pl.loop(0, HIT_CAP // HIT_GROUP)
    def _(i):
        acc = shares[...]
        for j in range(HIT_GROUP):
            h = i * HIT_GROUP + j
            s = jnp.clip(jnp.sum(jnp.where(rank == h.astype(F32), linear, 0)), 0, NA * NB * SLOTS - 1)
            hits_ref[h + 1] = s
            goal = ((s // SLOTS) % NB) * 128 + (s // (SLOTS * NB)) * SLOTS + s % SLOTS
            value = share_of(s, h < count, spos_ref, e_ref, a, b, lane_z)
            acc = acc + jnp.where(linear == goal, value, 0.0)
        shares[...] = acc

    for j in range(NB):
        c_out[j, 0:1, :] = shares[j : j + 1, :]
        c_out[j, 1:2, :] = jnp.full((1, 128), over, I32).astype(F32)

    pl.semaphore_wait(barrier, len(az) + len(ax))

    for i, peer in enumerate(az):
        pltpu.make_async_remote_copy(
            c_out.at[peer[1]], c1.at[b], s1s, s1r, device_id=peer, device_id_type=MESH
        ).start()
    c1[b] = c_out[b]

    @pl.loop(0, CX)
    def _(x):
        t = thermal_distribution(e_ref[x])
        t_ref[x] = t
        ty[0, x] = t[0:1]
        ty[1, x] = t[CY - 1 : CY]

    up_b, down_b = (a, lax.rem(b + 1, NB)), (a, lax.rem(b + NB - 1, NB))
    up_a, down_a = (lax.rem(a + 1, NA), b), (lax.rem(a + NA - 1, NA), b)
    y_up = pltpu.make_async_remote_copy(ty.at[1], hy.at[0], hys.at[0], hyr.at[0], device_id=up_b, device_id_type=MESH)
    y_down = pltpu.make_async_remote_copy(ty.at[0], hy.at[1], hys.at[1], hyr.at[1], device_id=down_b, device_id_type=MESH)
    y_up.start()
    y_down.start()

    load_p.wait()
    load_m.wait()
    to_smem.wait()

    @pl.loop(0, SLOTS)
    def _(s):
        p = p_ref[s].T
        m = m_ref[s].T * DT_PHASE
        for h in range(2):
            ph, mh = p[:, h * 128 : h * 128 + 128], m[:, h * 128 : h * 128 + 128]
            pt[s, h] = ph
            mt[s, h] = mh
            base = h * 12
            eb[2 * s, base : base + 6] = ph[0:6]
            eb[2 * s, base + 6 : base + 11] = mh[0:5]
            eb[2 * s + 1, base : base + 6] = ph[250:256]
            eb[2 * s + 1, base + 6 : base + 11] = mh[251:256]
            eb[2 * s, base + 11 : base + 12] = jnp.zeros((1, 128), F32)
            eb[2 * s + 1, base + 11 : base + 12] = jnp.zeros((1, 128), F32)

    @pl.loop(0, (NA - 1) * CAP)
    def _(n):
        sb[n] = eb[jnp.clip(send_ref[0, n], 0, 2 * SLOTS - 1)]

    whole1 = pltpu.make_async_remote_copy(
        c_out.at[pl.ds(0, NB - 1)], c1.at[pl.ds(0, NB - 1)], s1s, s1r, device_id=az[0], device_id_type=MESH
    )
    whole1.wait_recv()
    sum1[...] = jnp.sum(c1[...], axis=0)
    for i, peer in enumerate(ax):
        pltpu.make_async_remote_copy(sum1, c2.at[a], s2s, s2r, device_id=peer, device_id_type=MESH).start()
    c2[a] = sum1[...]

    for i, peer in enumerate(ax):
        pltpu.make_async_remote_copy(
            sb.at[pl.ds(i * CAP, CAP)], rb.at[pl.ds(i * CAP, CAP)], es, er, device_id=peer, device_id_type=MESH
        ).start()

    x_up = pltpu.make_async_remote_copy(
        t_ref.at[CX - 1], hx.at[0], hxs.at[0], hxr.at[0], device_id=up_a, device_id_type=MESH
    )
    x_down = pltpu.make_async_remote_copy(
        t_ref.at[0], hx.at[1], hxs.at[1], hxr.at[1], device_id=down_a, device_id_type=MESH
    )
    x_up.start()
    x_down.start()

    y_up.wait()
    y_down.wait()

    line = lax.broadcasted_iota(I32, (CY, CZ), 0)
    radial = lax.broadcasted_iota(I32, (CY, CZ), 1)

    def plane(x, below, above):
        t = t_ref[x]
        ym = jnp.where(line == 0, hy[0, x], pltpu.roll(t, 1, 0))
        yp = jnp.where(line == CY - 1, hy[1, x], pltpu.roll(t, CY - 1, 0))
        zm = jnp.where(radial == 0, 0.0, pltpu.roll(t, 1, 1))
        zp = jnp.where(radial == CZ - 1, 0.0, pltpu.roll(t, CZ - 1, 1))
        heated_ref[x] = e_ref[x] + DT_MACRO * ((below + above) + (ym + yp) + (zm + zp) - 6.0 * t)

    @pl.loop(1, CX - 1)
    def _(x):
        plane(x, t_ref[x - 1], t_ref[x + 1])

    whole2 = pltpu.make_async_remote_copy(
        c2.at[pl.ds(0, NA - 1)], c2.at[pl.ds(0, NA - 1)], s2s, s2r, device_id=ax[0], device_id_type=MESH
    )
    whole2.wait_recv()
    total = jnp.sum(c2[...], axis=0)
    over_ref[...] = total[1:2]
    temps = thermal_distribution(total[0:1])

    def temp_of(index):
        return jnp.sum(jnp.where(lanes1 == index, temps, 0.0), axis=1, keepdims=True)

    lane_full = lax.broadcasted_iota(I32, (SIDE, 128), 1)
    row_full = lax.broadcasted_iota(I32, (SIDE, 128), 0)
    body = (row_full >= 6) & (row_full < SIDE - 6)

    @pl.loop(0, SLOTS)
    def _(s):
        tau = temp_of(a * SLOTS + s)
        nb_t[s] = jnp.broadcast_to(tau, (1, 128))
        k1, k4 = 1.5 + DRIVE_GAIN * tau, 4.5 + DRIVE_GAIN * tau
        cur = (pt[s, 0], pt[s, 1])
        for _step in range(PHASE_STEPS):
            cur = phase_step(cur, (mt[s, 0], mt[s, 1]), k1, k4, lane_full)
        ct[s, 0] = cur[0]
        ct[s, 1] = cur[1]
        change = (cur[0] - pt[s, 0]) + (cur[1] - pt[s, 1])
        latsum[s] = jnp.sum(jnp.where(body, change, 0.0), axis=0, keepdims=True)

    whole_e = pltpu.make_async_remote_copy(sb, rb, es, er, device_id=ax[0], device_id_type=MESH)
    whole_e.wait_recv()
    lane_strip = lax.broadcasted_iota(I32, (24, 128), 1)
    row_strip = lax.broadcasted_iota(I32, (24, 128), 0)
    lat[...] = jnp.zeros((1, 128), F32)

    @pl.loop(0, SLOTS)
    def _(s):
        tau = nb_t[s]
        curs, rates, ks = [], [], []
        for side in range(2):
            e = 2 * s + side
            own_edge = place_ref[3 * e + 1]
            near = eb[own_edge]
            far = rb[recv_ref[e]]
            is_far = jnp.broadcast_to(place_ref[3 * e + 2], (EDGE_ROWS, 128)) > 0
            edge = jnp.where(is_far, far, near)
            other = temp_of(place_ref[3 * e])
            for h in range(2):
                ph, mh = edge[h * 12 : h * 12 + 6], edge[h * 12 + 6 : h * 12 + 11]
                if side == 0:
                    stp[side, h, 0:2] = jnp.zeros((2, 128), F32)
                    stp[side, h, 2:8] = ph
                    stp[side, h, 8:24] = pt[s, h, 0:16]
                    stm[side, h, 0:3] = jnp.zeros((3, 128), F32)
                    stm[side, h, 3:8] = mh
                    stm[side, h, 8:24] = mt[s, h, 0:16]
                else:
                    stp[side, h, 0:16] = pt[s, h, SIDE - 16 : SIDE]
                    stp[side, h, 16:22] = ph
                    stp[side, h, 22:24] = jnp.zeros((2, 128), F32)
                    stm[side, h, 0:16] = mt[s, h, SIDE - 16 : SIDE]
                    stm[side, h, 16:21] = mh
                    stm[side, h, 21:24] = jnp.zeros((3, 128), F32)
            outer = row_strip < 8 if side == 0 else row_strip >= 16
            ks.append(DRIVE_GAIN * jnp.where(outer, other, tau))
            curs.append((stp[side, 0], stp[side, 1]))
            rates.append((stm[side, 0], stm[side, 1]))
        starts = curs
        for _step in range(PHASE_STEPS):
            curs = [
                phase_step(curs[side], rates[side], 1.5 + ks[side], 4.5 + ks[side], lane_strip) for side in range(2)
            ]
        total_s = latsum[s]
        for side in range(2):
            low = 8 if side == 0 else 10
            first = 0 if side == 0 else SIDE - 6
            for h in range(2):
                ct[s, h, first : first + 6] = curs[side][h][low : low + 6]
            kept = (row_strip >= low) & (row_strip < low + 6)
            change = (curs[side][0] - starts[side][0]) + (curs[side][1] - starts[side][1])
            total_s = total_s + jnp.sum(jnp.where(kept, change, 0.0), axis=0, keepdims=True)
        value = jnp.sum(total_s, axis=1, keepdims=True) * (COUPLING / (SIDE * SIDE))
        lat[...] = jnp.where(lanes1 == a * SLOTS + s, jnp.where(alive_all > 0.5, value, 0.0), lat[...])

    for i, peer in enumerate(ax):
        pltpu.make_async_remote_copy(lat, l1.at[a], l1s, l1r, device_id=peer, device_id_type=MESH).start()
    l1[a] = lat[...]

    x_up.wait()
    x_down.wait()
    plane(0, jnp.where(a > 0, 1.0, 0.0).astype(F32) * hx[0], t_ref[1])
    plane(CX - 1, t_ref[CX - 2], jnp.where(a < NA - 1, 1.0, 0.0).astype(F32) * hx[1])

    whole_l1 = pltpu.make_async_remote_copy(
        l1.at[pl.ds(0, NA - 1)], l1.at[pl.ds(0, NA - 1)], l1s, l1r, device_id=ax[0], device_id_type=MESH
    )
    whole_l1.wait_recv()
    column = jnp.sum(l1[...], axis=0)
    l2[b] = column
    for i, peer in enumerate(az):
        pltpu.make_async_remote_copy(l2.at[b], l2.at[b], l2s, l2r, device_id=peer, device_id_type=MESH).start()

    @pl.loop(0, SLOTS)
    def _(s):
        alive = jnp.sum(jnp.where(lanes1 == a * SLOTS + s, alive_all, 0.0), axis=1, keepdims=True)
        for h in range(2):
            final = jnp.where(alive > 0.5, ct[s, h], pt[s, h])
            out_ref[s, h * 128 : h * 128 + 128, :] = final.T

    whole_l2 = pltpu.make_async_remote_copy(
        l2.at[pl.ds(0, NB - 1)], l2.at[pl.ds(0, NB - 1)], l2s, l2r, device_id=az[0], device_id_type=MESH
    )
    whole_l2.wait_recv()
    for j in range(NB):
        latent_ref[j : j + 1, :] = l2[j]

    whole1.wait_send()
    whole2.wait_send()
    whole_e.wait_send()
    whole_l1.wait_send()
    whole_l2.wait_send()


def release_kernel(hits_ref, spos_ref, lat_ref, heated_hbm, phase_hbm, out_hbm, phase_out_hbm, grid_ref, sem):
    move = pltpu.make_async_copy(phase_hbm, phase_out_hbm, sem.at[0])
    move.start()
    load = pltpu.make_async_copy(heated_hbm, grid_ref, sem.at[1])
    load.start()
    a, b = lax.axis_index("axial"), lax.axis_index("azim")
    lane = lax.broadcasted_iota(I32, (1, CZ), 1)
    load.wait()

    def add(h, carry):
        s = hits_ref[h + 1]
        px, py = local_cell(spos_ref[0, s], spos_ref[1, s], a, b)
        z = spos_ref[2, s]
        inside = (px >= 0) & (px < CX) & (py >= 0) & (py < CY)
        x0 = jnp.clip(px, 0, CX - 1)
        y0 = jnp.clip(py, 0, CY - 1)
        lat = lat_ref[((s // SLOTS) % NB) * 128 + (s // (SLOTS * NB)) * SLOTS + s % SLOTS]
        value = jnp.where(inside, lat, 0.0)
        grid_ref[x0, pl.ds(y0, 1), :] = grid_ref[x0, pl.ds(y0, 1), :] + jnp.where(lane == z, value, 0.0)
        return carry

    lax.fori_loop(0, hits_ref[0], add, 0)
    store = pltpu.make_async_copy(grid_ref, out_hbm, sem.at[2])
    store.start()
    store.wait()
    move.wait()


def spec(space):
    return pl.BlockSpec(memory_space=space)


def shards(specific_heat_content, phase, mobility, positions, counts, neighbours):
    pos = positions.T
    near = neighbours.T

    heated, phase_new, latents, over_all, hits = pl.pallas_call(
        main_kernel,
        out_shape=(
            jax.ShapeDtypeStruct((CX, CY, CZ), F32),
            jax.ShapeDtypeStruct((SLOTS, SIDE, SIDE), F32),
            jax.ShapeDtypeStruct((NB, 128), F32),
            jax.ShapeDtypeStruct((1, 128), F32),
            jax.ShapeDtypeStruct((HIT_CAP + 8,), I32),
        ),
        in_specs=[spec(VMEM)] + [spec(SMEM)] * 3 + [spec(pl.ANY)] * 3,
        out_specs=(spec(VMEM), spec(VMEM), spec(VMEM), spec(VMEM), spec(SMEM)),
        scratch_shapes=[
            VMEM((1, 128), I32),
            SMEM((1, 128), I32),
            SMEM((2 * SLOTS,), I32),
            SMEM((6 * SLOTS,), I32),
            VMEM((2, NB, 128), I32),
            VMEM((NB, 128), F32),
            VMEM((CX, CY, CZ), F32),
            VMEM((CX, CY, CZ), F32),
            VMEM((SLOTS, SIDE, SIDE), F32),
            VMEM((SLOTS, SIDE, SIDE), F32),
            VMEM((SLOTS, 2, SIDE, 128), F32),
            VMEM((SLOTS, 2, SIDE, 128), F32),
            VMEM((SLOTS, 2, SIDE, 128), F32),
            VMEM((2 * SLOTS, EDGE_ROWS, 128), F32),
            VMEM(((NA - 1) * CAP, EDGE_ROWS, 128), F32),
            VMEM(((NA - 1) * CAP, EDGE_ROWS, 128), F32),
            VMEM((2, 2, 24, 128), F32),
            VMEM((2, 2, 24, 128), F32),
            VMEM((2, CY, CZ), F32),
            VMEM((2, CX, 1, CZ), F32),
            VMEM((2, CX, 1, CZ), F32),
            VMEM((NB, 2, 128), F32),
            VMEM((NB, 2, 128), F32),
            VMEM((NA, 2, 128), F32),
            VMEM((2, 128), F32),
            VMEM((1, 128), F32),
            VMEM((NA, 1, 128), F32),
            VMEM((NB, 1, 128), F32),
            VMEM((SLOTS, 1, 128), F32),
            VMEM((SLOTS, 1, 128), F32),
            DMA((4,)),
            DMA, DMA, DMA, DMA, DMA, DMA,
            DMA((2,)), DMA((2,)), DMA((2,)), DMA((2,)),
            DMA, DMA, DMA, DMA,
        ],
        compiler_params=pltpu.CompilerParams(
            collective_id=0, has_side_effects=True, vmem_limit_bytes=48 << 20
        ),
        name="couple",
    )(pos, pos, near, counts, specific_heat_content, phase, mobility)

    def finish():
        return pl.pallas_call(
            release_kernel,
            out_shape=(
                jax.ShapeDtypeStruct((CX, CY, CZ), F32),
                jax.ShapeDtypeStruct((SLOTS, SIDE, SIDE), F32),
            ),
            in_specs=[spec(SMEM)] * 3 + [spec(pl.ANY)] * 2,
            out_specs=(spec(pl.ANY), spec(pl.ANY)),
            scratch_shapes=[VMEM((CX, CY, CZ), F32), DMA((3,))],
            compiler_params=pltpu.CompilerParams(vmem_limit_bytes=16 << 20),
            name="release",
        )(hits, pos, latents.reshape(-1), heated, phase_new)

    def whole():
        return general(specific_heat_content, phase, mobility, positions, counts, neighbours)

    return lax.cond(over_all[0, 0] > 0.5, whole, finish)


def solution(mesh):
    in_specs = (
        P("axial", "azim", None),
        P(("axial", "azim"), None, None),
        P(("axial", "azim"), None, None),
        P(),
        P(("axial", "azim")),
        P(("axial", "azim"), None),
    )
    out_specs = (P("axial", "azim", None), P(("axial", "azim"), None, None))
    return jax.shard_map(shards, mesh=mesh, in_specs=in_specs, out_specs=out_specs, check_vma=False)
```

```python
import jax
import jax.numpy as jnp
from jax import lax
from jax.experimental import pallas as pl
from jax.experimental.pallas import tpu as pltpu
from jax.sharding import PartitionSpec as P

PHASE_STEPS = 6
DT_MACRO = 0.1
DT_PHASE = 0.1
LATENT_HEAT = 1.0
DRIVE_GAIN = 2.0
COUPLING = 20.0

NA = 16
NB = 8
SLOTS = 8
SIDE = 256
CX, CY, CZ = 16, 128, 512
CAP = 5
HIT_CAP = 32
HIT_GROUP = 8
LANES = 128
STRIP_GROUP = 4
EDGE_ROWS = 24
MESH = pl.DeviceIdType.MESH
F32 = jnp.float32
I32 = jnp.int32
VMEM = pltpu.VMEM
SMEM = pltpu.SMEM
DMA = pltpu.SemaphoreType.DMA


def extended(value, sides, width, wrap):
    for axis, dim in sides:
        size, length = (lax.axis_size(axis), value.shape[dim])
        up = [(i, (i + 1) % size) for i in range(size if wrap else size - 1)]
        down = [(j, i) for i, j in up]
        last = lax.slice_in_dim(value, length - width, length, axis=dim)
        initial = lax.slice_in_dim(value, 0, width, axis=dim)
        before = lax.ppermute(last, axis, up)
        after = lax.ppermute(initial, axis, down)
        value = jnp.concatenate([before, value, after], axis=dim)
    return value


def thermal_distribution(quantity_lines):
    return jnp.minimum(quantity_lines, 0.0) + jnp.maximum(quantity_lines - LATENT_HEAT, 0.0)


def advance(current, mobility, drive, column_pad):
    solid_row = jnp.ones_like(current[:, :1, :])
    liquid_row = jnp.zeros_like(current[:, :1, :])
    row_pad = jnp.concatenate([solid_row, current, liquid_row], axis=1)
    diffusion_operator = (
        row_pad[:, :-2]
        + row_pad[:, 2:]
        + column_pad[:, :, :-2]
        + column_pad[:, :, 2:]
        - 4.0 * current
    )
    reaction = current * (1.0 - current) * (current - 0.5 - DRIVE_GAIN * drive)
    return current + DT_PHASE * mobility * (diffusion_operator + reaction)


def general(specific_heat_content, phase, mobility, positions, counts, neighbours):
    thermal_lines = thermal_distribution(specific_heat_content)
    lengthwise_margin = extended(thermal_lines, (("axial", 0),), 1, False)
    angular_margin = extended(thermal_lines, (("azim", 1),), 1, True)
    spoke_margin = jnp.pad(thermal_lines, ((0, 0), (0, 0), (1, 1)))
    diffusion_operator = (
        lengthwise_margin[2:]
        + lengthwise_margin[:-2]
        + angular_margin[:, 2:]
        + angular_margin[:, :-2]
        + spoke_margin[:, :, 2:]
        + spoke_margin[:, :, :-2]
        - 6.0 * thermal_lines
    )
    warmed_snapshot = specific_heat_content + DT_MACRO * diffusion_operator
    chilled_snapshot = thermal_distribution(warmed_snapshot)
    cells_x, cells_y, cells_z = specific_heat_content.shape
    local_x = positions[:, 0] - lax.axis_index("axial") * cells_x
    local_y = positions[:, 1] - lax.axis_index("azim") * cells_y
    inside = (local_x >= 0) & (local_x < cells_x) & (local_y >= 0) & (local_y < cells_y)
    flat_index = (
        jnp.clip(local_x, 0, cells_x - 1) * (cells_y * cells_z)
        + jnp.clip(local_y, 0, cells_y - 1) * cells_z
        + positions[:, 2]
    )
    sampled = jnp.where(inside, chilled_snapshot.reshape(-1)[flat_index], 0.0)
    patch_temps = lax.psum_scatter(sampled, ("axial", "azim"), scatter_dimension=0, tiled=True)
    capacity = phase.shape[0]
    live_slots = jnp.arange(capacity, dtype=jnp.int32) < counts[0]
    azim_count = lax.axis_size("azim")
    prev_rows = neighbours[:, 0] // capacity // azim_count * capacity + neighbours[:, 0] % capacity
    next_rows = neighbours[:, 1] // capacity // azim_count * capacity + neighbours[:, 1] % capacity
    drive = patch_temps[:, None, None]
    current = phase
    for iteration in range(PHASE_STEPS):
        edges = jnp.stack([current[:, :, 0], current[:, :, -1]], axis=1)
        gathered = lax.all_gather(edges, "axial", axis=0, tiled=True)
        left_edge = gathered[prev_rows, 1]
        right_edge = gathered[next_rows, 0]
        column_pad = jnp.concatenate(
            [left_edge[:, :, None], current, right_edge[:, :, None]], axis=2
        )
        current = advance(current, mobility, drive, column_pad)
    latent = jnp.where(live_slots, COUPLING * jnp.mean(current - phase, axis=(1, 2)), 0.0)
    phase_out = jnp.where(live_slots[:, None, None], current, phase)
    all_latent = lax.all_gather(latent, ("axial", "azim"), axis=0, tiled=True)
    released = jnp.where(inside, all_latent, 0.0)
    enthalpy_out = (
        warmed_snapshot.reshape(-1)
        .at[flat_index]
        .add(released)
        .reshape(specific_heat_content.shape)
    )
    return (enthalpy_out, phase_out)


def local_cell(x, y, a, b):
    return x - a * CX, ((y - b * CY + 1) & (NB * CY - 1)) - 1


def rank_hits(pos_ref, posb, a, b):
    for c in range(2):
        for r in range(8):
            posb[c, r : r + 1, :] = pos_ref[c : c + 1, r * 128 : r * 128 + 128]
    lx, ly = local_cell(posb[0], posb[1], a, b)
    inx = (lx >= 0) & (lx < CX)
    iny = (ly >= 0) & (ly < CY)
    touched = (inx & (ly <= CY)) | (iny & (lx >= -1) & (lx <= CX))
    mark = jnp.where(touched, 1.0, 0.0).astype(F32)
    row = lax.broadcasted_iota(I32, (128, 128), 0)
    col = lax.broadcasted_iota(I32, (128, 128), 1)
    before = jnp.where(row < col, 1.0, 0.0).astype(F32)
    within = jnp.dot(mark, before, preferred_element_type=F32)
    totals = jnp.dot(mark, jnp.ones((128, 128), F32), preferred_element_type=F32)
    row8 = lax.broadcasted_iota(I32, (8, 8), 0)
    col8 = lax.broadcasted_iota(I32, (8, 8), 1)
    above = jnp.dot(jnp.where(col8 < row8, 1.0, 0.0).astype(F32), totals, preferred_element_type=F32)
    rank = jnp.where(touched, within + above, -1.0)
    return rank, jnp.sum(touched.astype(I32))


def share_of(s, valid, spos_ref, e_ref, a, b, lane_z):
    px, py = local_cell(spos_ref[0, s], spos_ref[1, s], a, b)
    z = spos_ref[2, s]
    okx = (px >= 0) & (px < CX) & valid
    oky = (py >= 0) & (py < CY) & valid
    x0 = jnp.clip(px, 0, CX - 1)
    y0 = jnp.clip(py, 0, CY - 1)

    def part(x, y, ok):
        x, y = jnp.clip(x, 0, CX - 1), jnp.clip(y, 0, CY - 1)
        t = thermal_distribution(e_ref[x, pl.ds(y, 1), :])
        return jnp.where(ok, t, 0.0)

    own = jnp.where(okx & oky, e_ref[x0, pl.ds(y0, 1), :], 0.0)
    t = thermal_distribution(own)
    ring = (
        part(px - 1, y0, oky & (px >= 1) & (px <= CX))
        + part(px + 1, y0, oky & (px >= -1) & (px < CX - 1))
        + part(x0, py - 1, okx & (py >= 1) & (py <= CY))
        + part(x0, py + 1, okx & (py >= -1) & (py < CY - 1))
    )
    beside = (lane_z == z - 1) | (lane_z == z + 1)
    line = jnp.where(lane_z == z, own + DT_MACRO * (ring - 6.0 * t), 0.0) + jnp.where(beside, DT_MACRO * t, 0.0)
    return (line[:, 0:128] + line[:, 128:256]) + (line[:, 256:384] + line[:, 384:512])


def seam_tables(nb_ref, place_ref, recv_ref, a):
    halos = range(2 * SLOTS)
    names = [nb_ref[e % 2, e // 2] for e in halos]
    source = [n // (SLOTS * NB) for n in names]
    slot = [n % SLOTS for n in names]
    over = jnp.int32(0)
    for e in halos:
        rank = jnp.int32(0)
        for f in range(e):
            rank = rank + (source[f] == source[e]).astype(I32)
        hop = (a - source[e] + NA) % NA
        far = (hop > 0).astype(I32)
        over = jnp.maximum(over, far * (rank >= CAP).astype(I32))
        recv_ref[e] = jnp.where(hop > 0, (hop - 1) * CAP + jnp.minimum(rank, CAP - 1), 0)
        place_ref[3 * e] = source[e] * SLOTS + slot[e]
        place_ref[3 * e + 1] = 2 * slot[e] + 1 - e % 2
        place_ref[3 * e + 2] = far
    key = [2 * slot[f] + 1 - f % 2 for f in halos]
    lane = lax.broadcasted_iota(I32, (1, 128), 1)
    sends = jnp.zeros((1, 128), I32)
    for f in halos:
        turn = jnp.int32(0)
        for g in halos:
            if g != f:
                turn = turn + ((source[g] == source[f]) & (key[g] < key[f])).astype(I32)
        hop = (source[f] - a + NA) % NA
        goal = jnp.where((hop > 0) & (turn < CAP), (hop - 1) * CAP + turn, -1)
        sends = sends + jnp.where(lane == goal, f, 0)
    return sends, over


def along_rows(halves, lane):
    even, odd = halves
    axis = even.ndim - 1
    above = jnp.where(lane == 0, 1.0, pltpu.roll(odd, 1, axis))
    below = jnp.where(lane == LANES - 1, 0.0, pltpu.roll(even, LANES - 1, axis))
    return above + odd, even + below


def along_columns(c):
    n = c.shape[0]
    first = pltpu.roll(c[n - 1], 1, 0)[None]
    last = pltpu.roll(c[0], 7, 0)[None]
    return jnp.concatenate([first, c[: n - 1]], axis=0) + jnp.concatenate([c[1:], last], axis=0)


def phase_step(halves, rates, k1, k4, lane):
    beside = along_rows(halves, lane)
    out = []
    for h in range(2):
        c = halves[h]
        out.append(c + rates[h] * ((beside[h] + along_columns(c)) + c * (c * (k1 - c) - k4)))
    return tuple(out)


def main_kernel(
    pos_ref, spos_ref, nb_ref, count_ref, e_hbm, phase_hbm, mob_hbm,
    heated_ref, out_ref, latent_ref, over_ref, hits_ref,
    send_v, send_ref, recv_ref, place_ref, posb, shares,
    e_ref, t_ref, p_ref, m_ref, pt, mt, ct, eb, sb, rb, stp, stm,
    hx, hy, ty, c_out, c1, c2, sum1, lat, l1, l2, latsum, nb_t, weave, rows_v,
    load_sem, s1s, s1r, s2s, s2r, es, er, hxs, hxr, hys, hyr, l1s, l1r, l2s, l2r,
):
    a, b = lax.axis_index("axial"), lax.axis_index("azim")
    ax = [(lax.rem(a + i, NA), b) for i in range(1, NA)]
    az = [(a, lax.rem(b + i, NB)) for i in range(1, NB)]
    barrier = pltpu.get_barrier_semaphore()
    for peer in az + ax:
        pl.semaphore_signal(barrier, inc=1, device_id=peer, device_id_type=MESH)

    load_e = pltpu.make_async_copy(e_hbm, e_ref, load_sem.at[4])
    load_e.start()
    loads = []
    for k, (src, dst) in enumerate(((phase_hbm, p_ref), (mob_hbm, m_ref))):
        for tile in range(2):
            columns = pl.ds(tile * LANES, LANES)
            loads.append(pltpu.make_async_copy(src.at[:, :, columns], dst.at[:, tile], load_sem.at[2 * k + tile]))
    for load in loads:
        load.start()

    lanes1 = lax.broadcasted_iota(I32, (1, 128), 1)
    alive_all = ((lanes1 // SLOTS == a) & (lanes1 % SLOTS < count_ref[0])).astype(F32)
    sends, over = seam_tables(nb_ref, place_ref, recv_ref, a)
    send_v[...] = sends
    to_smem = pltpu.make_async_copy(send_v, send_ref, load_sem.at[5])
    to_smem.start()
    rank, count = rank_hits(pos_ref, posb, a, b)
    over = jnp.maximum(over, (count > HIT_CAP).astype(I32))
    hits_ref[0] = jnp.minimum(count, HIT_CAP)
    linear = lax.broadcasted_iota(I32, (NB, 128), 0) * 128 + lax.broadcasted_iota(I32, (NB, 128), 1)
    lane_z = lax.broadcasted_iota(I32, (1, CZ), 1)

    @pl.loop(0, HIT_CAP // HIT_GROUP)
    def _(i):
        for j in range(HIT_GROUP):
            h = i * HIT_GROUP + j
            s = jnp.sum(jnp.where(rank == h.astype(F32), linear, 0))
            hits_ref[h + 1] = jnp.clip(s, 0, NA * NB * SLOTS - 1)

    load_e.wait()

    @pl.loop(0, HIT_CAP // HIT_GROUP)
    def _(i):
        for j in range(HIT_GROUP):
            h = i * HIT_GROUP + j
            s = jnp.clip(hits_ref[h + 1], 0, NA * NB * SLOTS - 1)
            rows_v[pl.ds(h, 1), :] = share_of(s, h < count, spos_ref, e_ref, a, b, lane_z)

    values = jnp.sum(rows_v[...], axis=1, keepdims=True)
    acc = jnp.zeros((NB, 128), F32)
    for h in range(HIT_CAP):
        s = hits_ref[h + 1]
        goal = ((s // SLOTS) % NB) * 128 + (s // (SLOTS * NB)) * SLOTS + s % SLOTS
        acc = acc + jnp.where(linear == goal, values[h : h + 1], 0.0)
    shares[...] = acc

    c_out[0:NB, :] = shares[...]
    c_out[NB : NB + 1, :] = jnp.full((1, 128), over, I32).astype(F32)

    pl.semaphore_wait(barrier, len(az) + len(ax))

    for i, peer in enumerate(ax):
        pltpu.make_async_remote_copy(c_out, c1.at[a], s1s, s1r, device_id=peer, device_id_type=MESH).start()
    c1[a] = c_out[...]

    for load in loads:
        load.wait()
    to_smem.wait()

    @pl.loop(0, SLOTS)
    def _(s):
        for h in range(2):
            for tile in range(2):
                rows = pl.ds(h, LANES, stride=2)
                ph = p_ref[s, tile, rows, :].T
                mh = m_ref[s, tile, rows, :].T * DT_PHASE
                for i in range(4):
                    place = pl.ds(tile * 4 + i, 32, stride=8)
                    pt[s, h, place, :] = ph[i * 32 : i * 32 + 32]
                    mt[s, h, place, :] = mh[i * 32 : i * 32 + 32]
                e = 2 * s + tile
                base = h * 12
                if tile == 0:
                    eb[e, base : base + 6] = ph[0:6]
                    eb[e, base + 6 : base + 11] = mh[0:5]
                    stp[s, tile, h, 0:2] = jnp.zeros((2, 128), F32)
                    stp[s, tile, h, 8:24] = ph[0:16]
                    stm[s, tile, h, 0:3] = jnp.zeros((3, 128), F32)
                    stm[s, tile, h, 8:24] = mh[0:16]
                else:
                    eb[e, base : base + 6] = ph[122:128]
                    eb[e, base + 6 : base + 11] = mh[123:128]
                    stp[s, tile, h, 0:16] = ph[112:128]
                    stp[s, tile, h, 22:24] = jnp.zeros((2, 128), F32)
                    stm[s, tile, h, 0:16] = mh[112:128]
                    stm[s, tile, h, 21:24] = jnp.zeros((3, 128), F32)
                eb[e, base + 11 : base + 12] = jnp.zeros((1, 128), F32)

    @pl.loop(0, (NA - 1) * CAP)
    def _(n):
        sb[n] = eb[jnp.clip(send_ref[0, n], 0, 2 * SLOTS - 1)]

    @pl.loop(0, CX)
    def _(x):
        t = thermal_distribution(e_ref[x])
        t_ref[x] = t
        ty[0, x] = t[0:1]
        ty[1, x] = t[CY - 1 : CY]

    up_b, down_b = (a, lax.rem(b + 1, NB)), (a, lax.rem(b + NB - 1, NB))
    up_a, down_a = (lax.rem(a + 1, NA), b), (lax.rem(a + NA - 1, NA), b)
    y_up = pltpu.make_async_remote_copy(ty.at[1], hy.at[0], hys.at[0], hyr.at[0], device_id=up_b, device_id_type=MESH)
    y_down = pltpu.make_async_remote_copy(ty.at[0], hy.at[1], hys.at[1], hyr.at[1], device_id=down_b, device_id_type=MESH)
    y_up.start()
    y_down.start()

    whole1 = pltpu.make_async_remote_copy(
        c1.at[pl.ds(0, NA - 1)], c1.at[pl.ds(0, NA - 1)], s1s, s1r, device_id=ax[0], device_id_type=MESH
    )
    whole1.wait_recv()
    partial = jnp.sum(c1[...], axis=0)
    for j in range(NB):
        sum1[j, 0:1, :] = partial[j : j + 1]
        sum1[j, 1:2, :] = partial[NB : NB + 1]
    for i, peer in enumerate(az):
        pltpu.make_async_remote_copy(
            sum1.at[peer[1]], c2.at[b], s2s, s2r, device_id=peer, device_id_type=MESH
        ).start()
    c2[b] = sum1[b]

    for i, peer in enumerate(ax):
        pltpu.make_async_remote_copy(
            sb.at[pl.ds(i * CAP, CAP)], rb.at[pl.ds(i * CAP, CAP)], es, er, device_id=peer, device_id_type=MESH
        ).start()

    x_up = pltpu.make_async_remote_copy(
        t_ref.at[CX - 1], hx.at[0], hxs.at[0], hxr.at[0], device_id=up_a, device_id_type=MESH
    )
    x_down = pltpu.make_async_remote_copy(
        t_ref.at[0], hx.at[1], hxs.at[1], hxr.at[1], device_id=down_a, device_id_type=MESH
    )
    x_up.start()
    x_down.start()

    y_up.wait()
    y_down.wait()

    line = lax.broadcasted_iota(I32, (CY, CZ), 0)
    radial = lax.broadcasted_iota(I32, (CY, CZ), 1)

    def plane(x, below, above):
        t = t_ref[x]
        ym = jnp.where(line == 0, hy[0, x], pltpu.roll(t, 1, 0))
        yp = jnp.where(line == CY - 1, hy[1, x], pltpu.roll(t, CY - 1, 0))
        zm = jnp.where(radial == 0, 0.0, pltpu.roll(t, 1, 1))
        zp = jnp.where(radial == CZ - 1, 0.0, pltpu.roll(t, CZ - 1, 1))
        heated_ref[x] = e_ref[x] + DT_MACRO * ((below + above) + (ym + yp) + (zm + zp) - 6.0 * t)

    @pl.loop(1, CX - 1)
    def _(x):
        plane(x, t_ref[x - 1], t_ref[x + 1])

    whole2 = pltpu.make_async_remote_copy(
        c2.at[pl.ds(0, NB - 1)], c2.at[pl.ds(0, NB - 1)], s2s, s2r, device_id=az[0], device_id_type=MESH
    )
    whole2.wait_recv()
    total = jnp.sum(c2[...], axis=0)
    over_ref[...] = total[1:2]
    temps = thermal_distribution(total[0:1])

    def temp_of(index):
        return jnp.sum(jnp.where(lanes1 == index, temps, 0.0), axis=1, keepdims=True)

    cells = (SIDE // 8, 8, LANES)
    lane_full = lax.broadcasted_iota(I32, cells, 2)
    column = lax.broadcasted_iota(I32, cells, 1) * (SIDE // 8) + lax.broadcasted_iota(I32, cells, 0)
    body = (column >= 6) & (column < SIDE - 6)

    @pl.loop(0, SLOTS)
    def _(s):
        tau = temp_of(a * SLOTS + s)
        nb_t[s] = jnp.broadcast_to(tau, (1, 128))
        k1, k4 = 1.5 + DRIVE_GAIN * tau, 4.5 + DRIVE_GAIN * tau
        start = (pt[s, 0].reshape(cells), pt[s, 1].reshape(cells))
        rates = (mt[s, 0].reshape(cells), mt[s, 1].reshape(cells))
        cur = start
        for _step in range(PHASE_STEPS):
            cur = phase_step(cur, rates, k1, k4, lane_full)
        ct[s, 0] = cur[0].reshape(SIDE, LANES)
        ct[s, 1] = cur[1].reshape(SIDE, LANES)
        change = (cur[0] - start[0]) + (cur[1] - start[1])
        latsum[s] = jnp.sum(jnp.sum(jnp.where(body, change, 0.0), axis=0), axis=0, keepdims=True)

    whole_e = pltpu.make_async_remote_copy(sb, rb, es, er, device_id=ax[0], device_id_type=MESH)
    whole_e.wait_recv()

    @pl.loop(0, SLOTS)
    def _(s):
        for side in range(2):
            e = 2 * s + side
            near = eb[place_ref[3 * e + 1]]
            far = rb[recv_ref[e]]
            is_far = jnp.broadcast_to(place_ref[3 * e + 2], (EDGE_ROWS, 128)) > 0
            edge = jnp.where(is_far, far, near)
            for h in range(2):
                first = 2 if side == 0 else 16
                stp[s, side, h, first : first + 6] = edge[h * 12 : h * 12 + 6]
                first = 3 if side == 0 else 16
                stm[s, side, h, first : first + 5] = edge[h * 12 + 6 : h * 12 + 11]
            nb_t[SLOTS + e] = jnp.broadcast_to(temp_of(place_ref[3 * e]), (1, 128))

    strip = (3, 8, LANES)
    lane_strip = lax.broadcasted_iota(I32, strip, 2)
    row_strip = lax.broadcasted_iota(I32, strip, 1) * 3 + lax.broadcasted_iota(I32, strip, 0)
    lat[...] = jnp.zeros((1, 128), F32)

    def woven(ref, s, side, h):
        return jnp.stack([ref[s, side, h, pl.ds(j, 8, stride=3), :] for j in range(3)], axis=0)

    @pl.loop(0, SLOTS // STRIP_GROUP)
    def _(n):
        pairs = [(n * STRIP_GROUP + k, side) for k in range(STRIP_GROUP) for side in range(2)]
        curs, rates, ks = [], [], []
        for s, side in pairs:
            curs.append((woven(stp, s, side, 0), woven(stp, s, side, 1)))
            rates.append((woven(stm, s, side, 0), woven(stm, s, side, 1)))
            outer = row_strip < 8 if side == 0 else row_strip >= 16
            ks.append(DRIVE_GAIN * jnp.where(outer, nb_t[SLOTS + 2 * s + side][None], nb_t[s][None]))
        starts = curs
        for _step in range(PHASE_STEPS):
            curs = [phase_step(c, r, 1.5 + k, 4.5 + k, lane_strip) for c, r, k in zip(curs, rates, ks)]
        for k in range(STRIP_GROUP):
            s = n * STRIP_GROUP + k
            total_s = latsum[s]
            for side in range(2):
                q = 2 * k + side
                low = 8 if side == 0 else 10
                for h in range(2):
                    for j in range(3):
                        stp[s, side, h, pl.ds(j, 8, stride=3), :] = curs[q][h][j]
                    if side == 0:
                        ct[s, h, pl.ds(0, 6, stride=8), :] = stp[s, side, h, low : low + 6]
                    else:
                        ct[s, h, pl.ds(26 * 8 + 7, 6, stride=8), :] = stp[s, side, h, low : low + 6]
                kept = (row_strip >= low) & (row_strip < low + 6)
                change = (curs[q][0] - starts[q][0]) + (curs[q][1] - starts[q][1])
                total_s = total_s + jnp.sum(jnp.sum(jnp.where(kept, change, 0.0), axis=0), axis=0, keepdims=True)
            value = jnp.sum(total_s, axis=1, keepdims=True) * (COUPLING / (SIDE * SIDE))
            lat[...] = jnp.where(lanes1 == a * SLOTS + s, jnp.where(alive_all > 0.5, value, 0.0), lat[...])

    for i, peer in enumerate(ax):
        pltpu.make_async_remote_copy(lat, l1.at[a], l1s, l1r, device_id=peer, device_id_type=MESH).start()
    l1[a] = lat[...]

    x_up.wait()
    x_down.wait()
    plane(0, jnp.where(a > 0, 1.0, 0.0).astype(F32) * hx[0], t_ref[1])
    plane(CX - 1, t_ref[CX - 2], jnp.where(a < NA - 1, 1.0, 0.0).astype(F32) * hx[1])

    whole_l1 = pltpu.make_async_remote_copy(
        l1.at[pl.ds(0, NA - 1)], l1.at[pl.ds(0, NA - 1)], l1s, l1r, device_id=ax[0], device_id_type=MESH
    )
    whole_l1.wait_recv()
    column = jnp.sum(l1[...], axis=0)
    l2[b] = column
    for i, peer in enumerate(az):
        pltpu.make_async_remote_copy(l2.at[b], l2.at[b], l2s, l2r, device_id=peer, device_id_type=MESH).start()

    @pl.loop(0, SLOTS)
    def _(s):
        alive = jnp.sum(jnp.where(lanes1 == a * SLOTS + s, alive_all, 0.0), axis=1, keepdims=True)
        for h in range(2):
            for tile in range(2):
                parts = []
                for i in range(4):
                    place = pl.ds(tile * 4 + i, 32, stride=8)
                    parts.append(jnp.where(alive > 0.5, ct[s, h, place, :], pt[s, h, place, :]))
                weave[tile, pl.ds(h, LANES, stride=2), :] = jnp.concatenate(parts, axis=0).T
        for tile in range(2):
            out_ref[s, :, tile * LANES : tile * LANES + LANES] = weave[tile]

    whole_l2 = pltpu.make_async_remote_copy(
        l2.at[pl.ds(0, NB - 1)], l2.at[pl.ds(0, NB - 1)], l2s, l2r, device_id=az[0], device_id_type=MESH
    )
    whole_l2.wait_recv()
    for j in range(NB):
        latent_ref[j : j + 1, :] = l2[j]

    whole1.wait_send()
    whole2.wait_send()
    whole_e.wait_send()
    whole_l1.wait_send()
    whole_l2.wait_send()


def release_kernel(hits_ref, spos_ref, lat_ref, heated_hbm, phase_hbm, out_hbm, phase_out_hbm, grid_ref, sem):
    move = pltpu.make_async_copy(phase_hbm, phase_out_hbm, sem.at[0])
    move.start()
    load = pltpu.make_async_copy(heated_hbm, grid_ref, sem.at[1])
    load.start()
    a, b = lax.axis_index("axial"), lax.axis_index("azim")
    lane = lax.broadcasted_iota(I32, (1, CZ), 1)
    load.wait()

    def add(h, carry):
        s = hits_ref[h + 1]
        px, py = local_cell(spos_ref[0, s], spos_ref[1, s], a, b)
        z = spos_ref[2, s]
        inside = (px >= 0) & (px < CX) & (py >= 0) & (py < CY)
        x0 = jnp.clip(px, 0, CX - 1)
        y0 = jnp.clip(py, 0, CY - 1)
        lat = lat_ref[((s // SLOTS) % NB) * 128 + (s // (SLOTS * NB)) * SLOTS + s % SLOTS]
        value = jnp.where(inside, lat, 0.0)
        grid_ref[x0, pl.ds(y0, 1), :] = grid_ref[x0, pl.ds(y0, 1), :] + jnp.where(lane == z, value, 0.0)
        return carry

    lax.fori_loop(0, hits_ref[0], add, 0)
    store = pltpu.make_async_copy(grid_ref, out_hbm, sem.at[2])
    store.start()
    store.wait()
    move.wait()


def spec(space):
    return pl.BlockSpec(memory_space=space)


def shards(specific_heat_content, phase, mobility, positions, counts, neighbours):
    pos = positions.T
    near = neighbours.T

    heated, phase_new, latents, over_all, hits = pl.pallas_call(
        main_kernel,
        out_shape=(
            jax.ShapeDtypeStruct((CX, CY, CZ), F32),
            jax.ShapeDtypeStruct((SLOTS, SIDE, SIDE), F32),
            jax.ShapeDtypeStruct((NB, 128), F32),
            jax.ShapeDtypeStruct((1, 128), F32),
            jax.ShapeDtypeStruct((HIT_CAP + 8,), I32),
        ),
        in_specs=[spec(VMEM)] + [spec(SMEM)] * 3 + [spec(pl.ANY)] * 3,
        out_specs=(spec(VMEM), spec(VMEM), spec(VMEM), spec(VMEM), spec(SMEM)),
        scratch_shapes=[
            VMEM((1, 128), I32),
            SMEM((1, 128), I32),
            SMEM((2 * SLOTS,), I32),
            SMEM((6 * SLOTS,), I32),
            VMEM((2, NB, 128), I32),
            VMEM((NB, 128), F32),
            VMEM((CX, CY, CZ), F32),
            VMEM((CX, CY, CZ), F32),
            VMEM((SLOTS, 2, SIDE, LANES), F32),
            VMEM((SLOTS, 2, SIDE, LANES), F32),
            VMEM((SLOTS, 2, SIDE, 128), F32),
            VMEM((SLOTS, 2, SIDE, 128), F32),
            VMEM((SLOTS, 2, SIDE, 128), F32),
            VMEM((2 * SLOTS, EDGE_ROWS, 128), F32),
            VMEM(((NA - 1) * CAP, EDGE_ROWS, 128), F32),
            VMEM(((NA - 1) * CAP, EDGE_ROWS, 128), F32),
            VMEM((SLOTS, 2, 2, 24, 128), F32),
            VMEM((SLOTS, 2, 2, 24, 128), F32),
            VMEM((2, CY, CZ), F32),
            VMEM((2, CX, 1, CZ), F32),
            VMEM((2, CX, 1, CZ), F32),
            VMEM((NB + 1, 128), F32),
            VMEM((NA, NB + 1, 128), F32),
            VMEM((NB, 2, 128), F32),
            VMEM((NB, 2, 128), F32),
            VMEM((1, 128), F32),
            VMEM((NA, 1, 128), F32),
            VMEM((NB, 1, 128), F32),
            VMEM((SLOTS, 1, 128), F32),
            VMEM((3 * SLOTS, 1, 128), F32),
            VMEM((2, SIDE, LANES), F32),
            VMEM((HIT_CAP, LANES), F32),
            DMA((6,)),
            DMA, DMA, DMA, DMA, DMA, DMA,
            DMA((2,)), DMA((2,)), DMA((2,)), DMA((2,)),
            DMA, DMA, DMA, DMA,
        ],
        compiler_params=pltpu.CompilerParams(
            collective_id=0, has_side_effects=True, vmem_limit_bytes=48 << 20
        ),
        name="couple",
    )(pos, pos, near, counts, specific_heat_content, phase, mobility)

    def finish():
        return pl.pallas_call(
            release_kernel,
            out_shape=(
                jax.ShapeDtypeStruct((CX, CY, CZ), F32),
                jax.ShapeDtypeStruct((SLOTS, SIDE, SIDE), F32),
            ),
            in_specs=[spec(SMEM)] * 3 + [spec(pl.ANY)] * 2,
            out_specs=(spec(pl.ANY), spec(pl.ANY)),
            scratch_shapes=[VMEM((CX, CY, CZ), F32), DMA((3,))],
            compiler_params=pltpu.CompilerParams(vmem_limit_bytes=16 << 20),
            name="release",
        )(hits, pos, latents.reshape(-1), heated, phase_new)

    def whole():
        return general(specific_heat_content, phase, mobility, positions, counts, neighbours)

    return lax.cond(over_all[0, 0] > 0.5, whole, finish)


def solution(mesh):
    in_specs = (
        P("axial", "azim", None),
        P(("axial", "azim"), None, None),
        P(("axial", "azim"), None, None),
        P(),
        P(("axial", "azim")),
        P(("axial", "azim"), None),
    )
    out_specs = (P("axial", "azim", None), P(("axial", "azim"), None, None))
    return jax.shard_map(shards, mesh=mesh, in_specs=in_specs, out_specs=out_specs, check_vma=False)
```

```python
import jax
import jax.numpy as jnp
from jax import lax
from jax.experimental import pallas as pl
from jax.experimental.pallas import tpu as pltpu
from jax.sharding import PartitionSpec as P

PHASE_STEPS = 6
DT_MACRO = 0.1
DT_PHASE = 0.1
LATENT_HEAT = 1.0
DRIVE_GAIN = 2.0
COUPLING = 20.0

NA = 16
NB = 8
SLOTS = 8
SIDE = 256
CX, CY, CZ = 16, 128, 512
CAP = 5
HIT_CAP = 32
HIT_GROUP = 8
LANES = 128
STRIP_GROUP = 4
EDGE_ROWS = 22
MESH = pl.DeviceIdType.MESH
F32 = jnp.float32
I32 = jnp.int32
VMEM = pltpu.VMEM
SMEM = pltpu.SMEM
DMA = pltpu.SemaphoreType.DMA


def extended(value, sides, width, wrap):
    for axis, dim in sides:
        size, length = (lax.axis_size(axis), value.shape[dim])
        up = [(i, (i + 1) % size) for i in range(size if wrap else size - 1)]
        down = [(j, i) for i, j in up]
        last = lax.slice_in_dim(value, length - width, length, axis=dim)
        initial = lax.slice_in_dim(value, 0, width, axis=dim)
        before = lax.ppermute(last, axis, up)
        after = lax.ppermute(initial, axis, down)
        value = jnp.concatenate([before, value, after], axis=dim)
    return value


def thermal_distribution(quantity_lines):
    return jnp.minimum(quantity_lines, 0.0) + jnp.maximum(quantity_lines - LATENT_HEAT, 0.0)


def advance(current, mobility, drive, column_pad):
    solid_row = jnp.ones_like(current[:, :1, :])
    liquid_row = jnp.zeros_like(current[:, :1, :])
    row_pad = jnp.concatenate([solid_row, current, liquid_row], axis=1)
    diffusion_operator = (
        row_pad[:, :-2]
        + row_pad[:, 2:]
        + column_pad[:, :, :-2]
        + column_pad[:, :, 2:]
        - 4.0 * current
    )
    reaction = current * (1.0 - current) * (current - 0.5 - DRIVE_GAIN * drive)
    return current + DT_PHASE * mobility * (diffusion_operator + reaction)


def general(specific_heat_content, phase, mobility, positions, counts, neighbours):
    thermal_lines = thermal_distribution(specific_heat_content)
    lengthwise_margin = extended(thermal_lines, (("axial", 0),), 1, False)
    angular_margin = extended(thermal_lines, (("azim", 1),), 1, True)
    spoke_margin = jnp.pad(thermal_lines, ((0, 0), (0, 0), (1, 1)))
    diffusion_operator = (
        lengthwise_margin[2:]
        + lengthwise_margin[:-2]
        + angular_margin[:, 2:]
        + angular_margin[:, :-2]
        + spoke_margin[:, :, 2:]
        + spoke_margin[:, :, :-2]
        - 6.0 * thermal_lines
    )
    warmed_snapshot = specific_heat_content + DT_MACRO * diffusion_operator
    chilled_snapshot = thermal_distribution(warmed_snapshot)
    cells_x, cells_y, cells_z = specific_heat_content.shape
    local_x = positions[:, 0] - lax.axis_index("axial") * cells_x
    local_y = positions[:, 1] - lax.axis_index("azim") * cells_y
    inside = (local_x >= 0) & (local_x < cells_x) & (local_y >= 0) & (local_y < cells_y)
    flat_index = (
        jnp.clip(local_x, 0, cells_x - 1) * (cells_y * cells_z)
        + jnp.clip(local_y, 0, cells_y - 1) * cells_z
        + positions[:, 2]
    )
    sampled = jnp.where(inside, chilled_snapshot.reshape(-1)[flat_index], 0.0)
    patch_temps = lax.psum_scatter(sampled, ("axial", "azim"), scatter_dimension=0, tiled=True)
    capacity = phase.shape[0]
    live_slots = jnp.arange(capacity, dtype=jnp.int32) < counts[0]
    azim_count = lax.axis_size("azim")
    prev_rows = neighbours[:, 0] // capacity // azim_count * capacity + neighbours[:, 0] % capacity
    next_rows = neighbours[:, 1] // capacity // azim_count * capacity + neighbours[:, 1] % capacity
    drive = patch_temps[:, None, None]
    current = phase
    for iteration in range(PHASE_STEPS):
        edges = jnp.stack([current[:, :, 0], current[:, :, -1]], axis=1)
        gathered = lax.all_gather(edges, "axial", axis=0, tiled=True)
        left_edge = gathered[prev_rows, 1]
        right_edge = gathered[next_rows, 0]
        column_pad = jnp.concatenate(
            [left_edge[:, :, None], current, right_edge[:, :, None]], axis=2
        )
        current = advance(current, mobility, drive, column_pad)
    latent = jnp.where(live_slots, COUPLING * jnp.mean(current - phase, axis=(1, 2)), 0.0)
    phase_out = jnp.where(live_slots[:, None, None], current, phase)
    all_latent = lax.all_gather(latent, ("axial", "azim"), axis=0, tiled=True)
    released = jnp.where(inside, all_latent, 0.0)
    enthalpy_out = (
        warmed_snapshot.reshape(-1)
        .at[flat_index]
        .add(released)
        .reshape(specific_heat_content.shape)
    )
    return (enthalpy_out, phase_out)


def local_cell(x, y, a, b):
    return x - a * CX, ((y - b * CY + 1) & (NB * CY - 1)) - 1


def rank_hits(pos_ref, posb, a, b):
    for c in range(2):
        for r in range(8):
            posb[c, r : r + 1, :] = pos_ref[c : c + 1, r * 128 : r * 128 + 128]
    lx, ly = local_cell(posb[0], posb[1], a, b)
    inx = (lx >= 0) & (lx < CX)
    iny = (ly >= 0) & (ly < CY)
    touched = (inx & (ly <= CY)) | (iny & (lx >= -1) & (lx <= CX))
    mark = jnp.where(touched, 1.0, 0.0).astype(F32)
    row = lax.broadcasted_iota(I32, (128, 128), 0)
    col = lax.broadcasted_iota(I32, (128, 128), 1)
    before = jnp.where(row < col, 1.0, 0.0).astype(F32)
    within = jnp.dot(mark, before, preferred_element_type=F32)
    totals = jnp.dot(mark, jnp.ones((128, 128), F32), preferred_element_type=F32)
    row8 = lax.broadcasted_iota(I32, (8, 8), 0)
    col8 = lax.broadcasted_iota(I32, (8, 8), 1)
    above = jnp.dot(jnp.where(col8 < row8, 1.0, 0.0).astype(F32), totals, preferred_element_type=F32)
    rank = jnp.where(touched, within + above, -1.0)
    return rank, jnp.sum(touched.astype(I32))


def share_of(s, valid, spos_ref, e_ref, a, b, lane_z):
    px, py = local_cell(spos_ref[0, s], spos_ref[1, s], a, b)
    z = spos_ref[2, s]
    okx = (px >= 0) & (px < CX) & valid
    oky = (py >= 0) & (py < CY) & valid
    x0 = jnp.clip(px, 0, CX - 1)
    y0 = jnp.clip(py, 0, CY - 1)

    def part(x, y, ok):
        x, y = jnp.clip(x, 0, CX - 1), jnp.clip(y, 0, CY - 1)
        t = thermal_distribution(e_ref[x, pl.ds(y, 1), :])
        return jnp.where(ok, t, 0.0)

    own = jnp.where(okx & oky, e_ref[x0, pl.ds(y0, 1), :], 0.0)
    t = thermal_distribution(own)
    ring = (
        part(px - 1, y0, oky & (px >= 1) & (px <= CX))
        + part(px + 1, y0, oky & (px >= -1) & (px < CX - 1))
        + part(x0, py - 1, okx & (py >= 1) & (py <= CY))
        + part(x0, py + 1, okx & (py >= -1) & (py < CY - 1))
    )
    beside = (lane_z == z - 1) | (lane_z == z + 1)
    line = jnp.where(lane_z == z, own + DT_MACRO * (ring - 6.0 * t), 0.0) + jnp.where(beside, DT_MACRO * t, 0.0)
    return (line[:, 0:128] + line[:, 128:256]) + (line[:, 256:384] + line[:, 384:512])


def seam_tables(nb_ref, place_ref, recv_ref, a):
    halos = range(2 * SLOTS)
    names = [nb_ref[e % 2, e // 2] for e in halos]
    source = [n // (SLOTS * NB) for n in names]
    slot = [n % SLOTS for n in names]
    over = jnp.int32(0)
    for e in halos:
        rank = jnp.int32(0)
        for f in range(e):
            rank = rank + (source[f] == source[e]).astype(I32)
        hop = (a - source[e] + NA) % NA
        far = (hop > 0).astype(I32)
        over = jnp.maximum(over, far * (rank >= CAP).astype(I32))
        recv_ref[e] = jnp.where(hop > 0, (hop - 1) * CAP + jnp.minimum(rank, CAP - 1), 0)
        place_ref[3 * e] = source[e] * SLOTS + slot[e]
        place_ref[3 * e + 1] = 2 * slot[e] + 1 - e % 2
        place_ref[3 * e + 2] = far
    key = [2 * slot[f] + 1 - f % 2 for f in halos]
    lane = lax.broadcasted_iota(I32, (1, 128), 1)
    sends = jnp.zeros((1, 128), I32)
    for f in halos:
        turn = jnp.int32(0)
        for g in halos:
            if g != f:
                turn = turn + ((source[g] == source[f]) & (key[g] < key[f])).astype(I32)
        hop = (source[f] - a + NA) % NA
        goal = jnp.where((hop > 0) & (turn < CAP), (hop - 1) * CAP + turn, -1)
        sends = sends + jnp.where(lane == goal, f, 0)
    return sends, over


def along_rows(halves, lane):
    even, odd = halves
    axis = even.ndim - 1
    above = jnp.where(lane == 0, 1.0, pltpu.roll(odd, 1, axis))
    below = jnp.where(lane == LANES - 1, 0.0, pltpu.roll(even, LANES - 1, axis))
    return above + odd, even + below


def along_columns(c):
    n = c.shape[0]
    first = pltpu.roll(c[n - 1], 1, 0)[None]
    last = pltpu.roll(c[0], 7, 0)[None]
    return jnp.concatenate([first, c[: n - 1]], axis=0) + jnp.concatenate([c[1:], last], axis=0)


def phase_step(halves, rates, k1, k4, lane):
    beside = along_rows(halves, lane)
    out = []
    for h in range(2):
        c = halves[h]
        out.append(c + rates[h] * ((beside[h] + along_columns(c)) + c * (c * (k1 - c) - k4)))
    return tuple(out)


def main_kernel(
    pos_ref, spos_ref, nb_ref, count_ref, e_hbm, phase_hbm, mob_hbm,
    heated_ref, out_ref, latent_ref, over_ref, hits_ref,
    send_v, send_ref, recv_ref, place_ref, posb, shares,
    e_ref, t_ref, p_ref, m_ref, pt, mt, ct, eb, sb, rb, stp, stm,
    hx, hy, ty, c_out, c1, c2, sum1, lat, l1, l2, latsum, nb_t, weave, rows_v,
    load_sem, s1s, s1r, s2s, s2r, es, er, hxs, hxr, hys, hyr, l1s, l1r, l2s, l2r,
):
    a, b = lax.axis_index("axial"), lax.axis_index("azim")
    ax = [(lax.rem(a + i, NA), b) for i in range(1, NA)]
    az = [(a, lax.rem(b + i, NB)) for i in range(1, NB)]
    barrier = pltpu.get_barrier_semaphore()
    for peer in az + ax:
        pl.semaphore_signal(barrier, inc=1, device_id=peer, device_id_type=MESH)

    load_e = pltpu.make_async_copy(e_hbm, e_ref, load_sem.at[4])
    load_e.start()
    loads = []
    for k, (src, dst) in enumerate(((phase_hbm, p_ref), (mob_hbm, m_ref))):
        for tile in range(2):
            columns = pl.ds(tile * LANES, LANES)
            loads.append(pltpu.make_async_copy(src.at[:, :, columns], dst.at[:, tile], load_sem.at[2 * k + tile]))
    for load in loads:
        load.start()

    lanes1 = lax.broadcasted_iota(I32, (1, 128), 1)
    alive_all = ((lanes1 // SLOTS == a) & (lanes1 % SLOTS < count_ref[0])).astype(F32)
    sends, over = seam_tables(nb_ref, place_ref, recv_ref, a)
    send_v[...] = sends
    to_smem = pltpu.make_async_copy(send_v, send_ref, load_sem.at[5])
    to_smem.start()
    rank, count = rank_hits(pos_ref, posb, a, b)
    over = jnp.maximum(over, (count > HIT_CAP).astype(I32))
    hits_ref[0] = jnp.minimum(count, HIT_CAP)
    linear = lax.broadcasted_iota(I32, (NB, 128), 0) * 128 + lax.broadcasted_iota(I32, (NB, 128), 1)
    lane_z = lax.broadcasted_iota(I32, (1, CZ), 1)

    @pl.loop(0, HIT_CAP // HIT_GROUP)
    def _(i):
        for j in range(HIT_GROUP):
            h = i * HIT_GROUP + j
            s = jnp.sum(jnp.where(rank == h.astype(F32), linear, 0))
            hits_ref[h + 1] = jnp.clip(s, 0, NA * NB * SLOTS - 1)

    load_e.wait()

    @pl.loop(0, HIT_CAP // HIT_GROUP)
    def _(i):
        for j in range(HIT_GROUP):
            h = i * HIT_GROUP + j
            s = jnp.clip(hits_ref[h + 1], 0, NA * NB * SLOTS - 1)
            rows_v[pl.ds(h, 1), :] = share_of(s, h < count, spos_ref, e_ref, a, b, lane_z)

    values = jnp.sum(rows_v[...], axis=1, keepdims=True)
    acc = jnp.zeros((NB, 128), F32)
    for h in range(HIT_CAP):
        s = hits_ref[h + 1]
        goal = ((s // SLOTS) % NB) * 128 + (s // (SLOTS * NB)) * SLOTS + s % SLOTS
        acc = acc + jnp.where(linear == goal, values[h : h + 1], 0.0)
    shares[...] = acc

    c_out[0:NB, :] = shares[...]
    c_out[NB : NB + 1, :] = jnp.full((1, 128), over, I32).astype(F32)

    pl.semaphore_wait(barrier, len(az) + len(ax))

    for i, peer in enumerate(ax):
        pltpu.make_async_remote_copy(c_out, c1.at[a], s1s, s1r, device_id=peer, device_id_type=MESH).start()
    c1[a] = c_out[...]

    for load in loads:
        load.wait()
    to_smem.wait()

    @pl.loop(0, SLOTS)
    def _(s):
        for h in range(2):
            for tile in range(2):
                rows = pl.ds(h, LANES, stride=2)
                ph = p_ref[s, tile, rows, :].T
                mh = m_ref[s, tile, rows, :].T * DT_PHASE
                for i in range(4):
                    place = pl.ds(tile * 4 + i, 32, stride=8)
                    pt[s, h, place, :] = ph[i * 32 : i * 32 + 32]
                    mt[s, h, place, :] = mh[i * 32 : i * 32 + 32]
                e = 2 * s + tile
                base = h * 11
                if tile == 0:
                    eb[e, base : base + 6] = ph[0:6]
                    eb[e, base + 6 : base + 11] = mh[0:5]
                    stp[s, tile, h, 0:2] = jnp.zeros((2, 128), F32)
                    stp[s, tile, h, 8:24] = ph[0:16]
                    stm[s, tile, h, 0:3] = jnp.zeros((3, 128), F32)
                    stm[s, tile, h, 8:24] = mh[0:16]
                else:
                    eb[e, base : base + 6] = ph[122:128]
                    eb[e, base + 6 : base + 11] = mh[123:128]
                    stp[s, tile, h, 0:16] = ph[112:128]
                    stp[s, tile, h, 22:24] = jnp.zeros((2, 128), F32)
                    stm[s, tile, h, 0:16] = mh[112:128]
                    stm[s, tile, h, 21:24] = jnp.zeros((3, 128), F32)

    for i, peer in enumerate(ax):
        for n in range(i * CAP, (i + 1) * CAP):
            sb[n] = eb[jnp.clip(send_ref[0, n], 0, 2 * SLOTS - 1)]
        pltpu.make_async_remote_copy(
            sb.at[pl.ds(i * CAP, CAP)], rb.at[pl.ds(i * CAP, CAP)], es, er, device_id=peer, device_id_type=MESH
        ).start()

    @pl.loop(0, CX)
    def _(x):
        t = thermal_distribution(e_ref[x])
        t_ref[x] = t
        ty[0, x] = t[0:1]
        ty[1, x] = t[CY - 1 : CY]

    up_b, down_b = (a, lax.rem(b + 1, NB)), (a, lax.rem(b + NB - 1, NB))
    up_a, down_a = (lax.rem(a + 1, NA), b), (lax.rem(a + NA - 1, NA), b)
    y_up = pltpu.make_async_remote_copy(ty.at[1], hy.at[0], hys.at[0], hyr.at[0], device_id=up_b, device_id_type=MESH)
    y_down = pltpu.make_async_remote_copy(ty.at[0], hy.at[1], hys.at[1], hyr.at[1], device_id=down_b, device_id_type=MESH)
    y_up.start()
    y_down.start()

    whole1 = pltpu.make_async_remote_copy(
        c1.at[pl.ds(0, NA - 1)], c1.at[pl.ds(0, NA - 1)], s1s, s1r, device_id=ax[0], device_id_type=MESH
    )
    whole1.wait_recv()
    partial = jnp.sum(c1[...], axis=0)
    for j in range(NB):
        sum1[j, 0:1, :] = partial[j : j + 1]
        sum1[j, 1:2, :] = partial[NB : NB + 1]
    for i, peer in enumerate(az):
        pltpu.make_async_remote_copy(
            sum1.at[peer[1]], c2.at[b], s2s, s2r, device_id=peer, device_id_type=MESH
        ).start()
    c2[b] = sum1[b]

    x_up = pltpu.make_async_remote_copy(
        t_ref.at[CX - 1], hx.at[0], hxs.at[0], hxr.at[0], device_id=up_a, device_id_type=MESH
    )
    x_down = pltpu.make_async_remote_copy(
        t_ref.at[0], hx.at[1], hxs.at[1], hxr.at[1], device_id=down_a, device_id_type=MESH
    )
    x_up.start()
    x_down.start()

    y_up.wait()
    y_down.wait()

    line = lax.broadcasted_iota(I32, (CY, CZ), 0)
    radial = lax.broadcasted_iota(I32, (CY, CZ), 1)

    def plane(x, below, above):
        t = t_ref[x]
        ym = jnp.where(line == 0, hy[0, x], pltpu.roll(t, 1, 0))
        yp = jnp.where(line == CY - 1, hy[1, x], pltpu.roll(t, CY - 1, 0))
        zm = jnp.where(radial == 0, 0.0, pltpu.roll(t, 1, 1))
        zp = jnp.where(radial == CZ - 1, 0.0, pltpu.roll(t, CZ - 1, 1))
        heated_ref[x] = e_ref[x] + DT_MACRO * ((below + above) + (ym + yp) + (zm + zp) - 6.0 * t)

    @pl.loop(1, CX - 1)
    def _(x):
        plane(x, t_ref[x - 1], t_ref[x + 1])

    whole2 = pltpu.make_async_remote_copy(
        c2.at[pl.ds(0, NB - 1)], c2.at[pl.ds(0, NB - 1)], s2s, s2r, device_id=az[0], device_id_type=MESH
    )
    whole2.wait_recv()
    total = jnp.sum(c2[...], axis=0)
    over_ref[...] = total[1:2]
    temps = thermal_distribution(total[0:1])

    def temp_of(index):
        return jnp.sum(jnp.where(lanes1 == index, temps, 0.0), axis=1, keepdims=True)

    cells = (SIDE // 8, 8, LANES)
    lane_full = lax.broadcasted_iota(I32, cells, 2)
    column = lax.broadcasted_iota(I32, cells, 1) * (SIDE // 8) + lax.broadcasted_iota(I32, cells, 0)
    body = (column >= 6) & (column < SIDE - 6)

    @pl.loop(0, SLOTS)
    def _(s):
        tau = temp_of(a * SLOTS + s)
        nb_t[s] = jnp.broadcast_to(tau, (1, 128))
        k1, k4 = 1.5 + DRIVE_GAIN * tau, 4.5 + DRIVE_GAIN * tau
        start = (pt[s, 0].reshape(cells), pt[s, 1].reshape(cells))
        rates = (mt[s, 0].reshape(cells), mt[s, 1].reshape(cells))
        cur = start
        for _step in range(PHASE_STEPS):
            cur = phase_step(cur, rates, k1, k4, lane_full)
        ct[s, 0] = cur[0].reshape(SIDE, LANES)
        ct[s, 1] = cur[1].reshape(SIDE, LANES)
        change = (cur[0] - start[0]) + (cur[1] - start[1])
        latsum[s] = jnp.sum(jnp.sum(jnp.where(body, change, 0.0), axis=0), axis=0, keepdims=True)

    whole_e = pltpu.make_async_remote_copy(sb, rb, es, er, device_id=ax[0], device_id_type=MESH)
    whole_e.wait_recv()

    @pl.loop(0, SLOTS)
    def _(s):
        for side in range(2):
            e = 2 * s + side
            near = eb[place_ref[3 * e + 1]]
            far = rb[recv_ref[e]]
            is_far = jnp.broadcast_to(place_ref[3 * e + 2], (EDGE_ROWS, 128)) > 0
            edge = jnp.where(is_far, far, near)
            for h in range(2):
                first = 2 if side == 0 else 16
                stp[s, side, h, first : first + 6] = edge[h * 11 : h * 11 + 6]
                first = 3 if side == 0 else 16
                stm[s, side, h, first : first + 5] = edge[h * 11 + 6 : h * 11 + 11]
            nb_t[SLOTS + e] = jnp.broadcast_to(temp_of(place_ref[3 * e]), (1, 128))

    strip = (3, 8, LANES)
    lane_strip = lax.broadcasted_iota(I32, strip, 2)
    row_strip = lax.broadcasted_iota(I32, strip, 1) * 3 + lax.broadcasted_iota(I32, strip, 0)
    lat[...] = jnp.zeros((1, 128), F32)

    def woven(ref, s, side, h):
        return jnp.stack([ref[s, side, h, pl.ds(j, 8, stride=3), :] for j in range(3)], axis=0)

    @pl.loop(0, SLOTS // STRIP_GROUP)
    def _(n):
        pairs = [(n * STRIP_GROUP + k, side) for k in range(STRIP_GROUP) for side in range(2)]
        curs, rates, ks = [], [], []
        for s, side in pairs:
            curs.append((woven(stp, s, side, 0), woven(stp, s, side, 1)))
            rates.append((woven(stm, s, side, 0), woven(stm, s, side, 1)))
            outer = row_strip < 8 if side == 0 else row_strip >= 16
            ks.append(DRIVE_GAIN * jnp.where(outer, nb_t[SLOTS + 2 * s + side][None], nb_t[s][None]))
        starts = curs
        for _step in range(PHASE_STEPS):
            curs = [phase_step(c, r, 1.5 + k, 4.5 + k, lane_strip) for c, r, k in zip(curs, rates, ks)]
        for k in range(STRIP_GROUP):
            s = n * STRIP_GROUP + k
            total_s = latsum[s]
            for side in range(2):
                q = 2 * k + side
                low = 8 if side == 0 else 10
                for h in range(2):
                    for j in range(3):
                        stp[s, side, h, pl.ds(j, 8, stride=3), :] = curs[q][h][j]
                    if side == 0:
                        ct[s, h, pl.ds(0, 6, stride=8), :] = stp[s, side, h, low : low + 6]
                    else:
                        ct[s, h, pl.ds(26 * 8 + 7, 6, stride=8), :] = stp[s, side, h, low : low + 6]
                kept = (row_strip >= low) & (row_strip < low + 6)
                change = (curs[q][0] - starts[q][0]) + (curs[q][1] - starts[q][1])
                total_s = total_s + jnp.sum(jnp.sum(jnp.where(kept, change, 0.0), axis=0), axis=0, keepdims=True)
            value = jnp.sum(total_s, axis=1, keepdims=True) * (COUPLING / (SIDE * SIDE))
            lat[...] = jnp.where(lanes1 == a * SLOTS + s, jnp.where(alive_all > 0.5, value, 0.0), lat[...])

    for i, peer in enumerate(ax):
        pltpu.make_async_remote_copy(lat, l1.at[a], l1s, l1r, device_id=peer, device_id_type=MESH).start()
    l1[a] = lat[...]

    x_up.wait()
    x_down.wait()
    plane(0, jnp.where(a > 0, 1.0, 0.0).astype(F32) * hx[0], t_ref[1])
    plane(CX - 1, t_ref[CX - 2], jnp.where(a < NA - 1, 1.0, 0.0).astype(F32) * hx[1])

    whole_l1 = pltpu.make_async_remote_copy(
        l1.at[pl.ds(0, NA - 1)], l1.at[pl.ds(0, NA - 1)], l1s, l1r, device_id=ax[0], device_id_type=MESH
    )
    whole_l1.wait_recv()
    column = jnp.sum(l1[...], axis=0)
    l2[b] = column
    for i, peer in enumerate(az):
        pltpu.make_async_remote_copy(l2.at[b], l2.at[b], l2s, l2r, device_id=peer, device_id_type=MESH).start()

    @pl.loop(0, SLOTS)
    def _(s):
        alive = jnp.sum(jnp.where(lanes1 == a * SLOTS + s, alive_all, 0.0), axis=1, keepdims=True)
        for h in range(2):
            for tile in range(2):
                parts = []
                for i in range(4):
                    place = pl.ds(tile * 4 + i, 32, stride=8)
                    parts.append(jnp.where(alive > 0.5, ct[s, h, place, :], pt[s, h, place, :]))
                weave[tile, pl.ds(h, LANES, stride=2), :] = jnp.concatenate(parts, axis=0).T
        for tile in range(2):
            out_ref[s, :, tile * LANES : tile * LANES + LANES] = weave[tile]

    whole_l2 = pltpu.make_async_remote_copy(
        l2.at[pl.ds(0, NB - 1)], l2.at[pl.ds(0, NB - 1)], l2s, l2r, device_id=az[0], device_id_type=MESH
    )
    whole_l2.wait_recv()
    for j in range(NB):
        latent_ref[j : j + 1, :] = l2[j]

    whole1.wait_send()
    whole2.wait_send()
    whole_e.wait_send()
    whole_l1.wait_send()
    whole_l2.wait_send()


def release_kernel(hits_ref, spos_ref, lat_ref, heated_hbm, phase_hbm, out_hbm, phase_out_hbm, grid_ref, sem):
    move = pltpu.make_async_copy(phase_hbm, phase_out_hbm, sem.at[0])
    move.start()
    load = pltpu.make_async_copy(heated_hbm, grid_ref, sem.at[1])
    load.start()
    a, b = lax.axis_index("axial"), lax.axis_index("azim")
    lane = lax.broadcasted_iota(I32, (1, CZ), 1)
    load.wait()

    def add(h, carry):
        s = hits_ref[h + 1]
        px, py = local_cell(spos_ref[0, s], spos_ref[1, s], a, b)
        z = spos_ref[2, s]
        inside = (px >= 0) & (px < CX) & (py >= 0) & (py < CY)
        x0 = jnp.clip(px, 0, CX - 1)
        y0 = jnp.clip(py, 0, CY - 1)
        lat = lat_ref[((s // SLOTS) % NB) * 128 + (s // (SLOTS * NB)) * SLOTS + s % SLOTS]
        value = jnp.where(inside, lat, 0.0)
        grid_ref[x0, pl.ds(y0, 1), :] = grid_ref[x0, pl.ds(y0, 1), :] + jnp.where(lane == z, value, 0.0)
        return carry

    lax.fori_loop(0, hits_ref[0], add, 0)
    store = pltpu.make_async_copy(grid_ref, out_hbm, sem.at[2])
    store.start()
    store.wait()
    move.wait()


def spec(space):
    return pl.BlockSpec(memory_space=space)


def shards(specific_heat_content, phase, mobility, positions, counts, neighbours):
    pos = positions.T
    near = neighbours.T

    heated, phase_new, latents, over_all, hits = pl.pallas_call(
        main_kernel,
        out_shape=(
            jax.ShapeDtypeStruct((CX, CY, CZ), F32),
            jax.ShapeDtypeStruct((SLOTS, SIDE, SIDE), F32),
            jax.ShapeDtypeStruct((NB, 128), F32),
            jax.ShapeDtypeStruct((1, 128), F32),
            jax.ShapeDtypeStruct((HIT_CAP + 8,), I32),
        ),
        in_specs=[spec(VMEM)] + [spec(SMEM)] * 3 + [spec(pl.ANY)] * 3,
        out_specs=(spec(VMEM), spec(VMEM), spec(VMEM), spec(VMEM), spec(SMEM)),
        scratch_shapes=[
            VMEM((1, 128), I32),
            SMEM((1, 128), I32),
            SMEM((2 * SLOTS,), I32),
            SMEM((6 * SLOTS,), I32),
            VMEM((2, NB, 128), I32),
            VMEM((NB, 128), F32),
            VMEM((CX, CY, CZ), F32),
            VMEM((CX, CY, CZ), F32),
            VMEM((SLOTS, 2, SIDE, LANES), F32),
            VMEM((SLOTS, 2, SIDE, LANES), F32),
            VMEM((SLOTS, 2, SIDE, 128), F32),
            VMEM((SLOTS, 2, SIDE, 128), F32),
            VMEM((SLOTS, 2, SIDE, 128), F32),
            VMEM((2 * SLOTS, EDGE_ROWS, 128), F32),
            VMEM(((NA - 1) * CAP, EDGE_ROWS, 128), F32),
            VMEM(((NA - 1) * CAP, EDGE_ROWS, 128), F32),
            VMEM((SLOTS, 2, 2, 24, 128), F32),
            VMEM((SLOTS, 2, 2, 24, 128), F32),
            VMEM((2, CY, CZ), F32),
            VMEM((2, CX, 1, CZ), F32),
            VMEM((2, CX, 1, CZ), F32),
            VMEM((NB + 1, 128), F32),
            VMEM((NA, NB + 1, 128), F32),
            VMEM((NB, 2, 128), F32),
            VMEM((NB, 2, 128), F32),
            VMEM((1, 128), F32),
            VMEM((NA, 1, 128), F32),
            VMEM((NB, 1, 128), F32),
            VMEM((SLOTS, 1, 128), F32),
            VMEM((3 * SLOTS, 1, 128), F32),
            VMEM((2, SIDE, LANES), F32),
            VMEM((HIT_CAP, LANES), F32),
            DMA((6,)),
            DMA, DMA, DMA, DMA, DMA, DMA,
            DMA((2,)), DMA((2,)), DMA((2,)), DMA((2,)),
            DMA, DMA, DMA, DMA,
        ],
        compiler_params=pltpu.CompilerParams(
            collective_id=0, has_side_effects=True, vmem_limit_bytes=48 << 20
        ),
        name="couple",
    )(pos, pos, near, counts, specific_heat_content, phase, mobility)

    def finish():
        return pl.pallas_call(
            release_kernel,
            out_shape=(
                jax.ShapeDtypeStruct((CX, CY, CZ), F32),
                jax.ShapeDtypeStruct((SLOTS, SIDE, SIDE), F32),
            ),
            in_specs=[spec(SMEM)] * 3 + [spec(pl.ANY)] * 2,
            out_specs=(spec(pl.ANY), spec(pl.ANY)),
            scratch_shapes=[VMEM((CX, CY, CZ), F32), DMA((3,))],
            compiler_params=pltpu.CompilerParams(vmem_limit_bytes=16 << 20),
            name="release",
        )(hits, pos, latents.reshape(-1), heated, phase_new)

    def whole():
        return general(specific_heat_content, phase, mobility, positions, counts, neighbours)

    return lax.cond(over_all[0, 0] > 0.5, whole, finish)


def solution(mesh):
    in_specs = (
        P("axial", "azim", None),
        P(("axial", "azim"), None, None),
        P(("axial", "azim"), None, None),
        P(),
        P(("axial", "azim")),
        P(("axial", "azim"), None),
    )
    out_specs = (P("axial", "azim", None), P(("axial", "azim"), None, None))
    return jax.shard_map(shards, mesh=mesh, in_specs=in_specs, out_specs=out_specs, check_vma=False)
```

```python
import jax
import jax.numpy as jnp
from jax import lax
from jax.experimental import pallas as pl
from jax.experimental.pallas import tpu as pltpu
from jax.sharding import PartitionSpec as P

PHASE_STEPS = 6
DT_MACRO = 0.1
DT_PHASE = 0.1
LATENT_HEAT = 1.0
DRIVE_GAIN = 2.0
COUPLING = 20.0

NA = 16
NB = 8
SLOTS = 8
SIDE = 256
CX, CY, CZ = 16, 128, 512
CAP = 5
HIT_CAP = 32
HIT_GROUP = 8
LANES = 128
STRIP_GROUP = 4
EDGE_ROWS = 22
MESH = pl.DeviceIdType.MESH
F32 = jnp.float32
I32 = jnp.int32
VMEM = pltpu.VMEM
SMEM = pltpu.SMEM
DMA = pltpu.SemaphoreType.DMA


def extended(value, sides, width, wrap):
    for axis, dim in sides:
        size, length = (lax.axis_size(axis), value.shape[dim])
        up = [(i, (i + 1) % size) for i in range(size if wrap else size - 1)]
        down = [(j, i) for i, j in up]
        last = lax.slice_in_dim(value, length - width, length, axis=dim)
        initial = lax.slice_in_dim(value, 0, width, axis=dim)
        before = lax.ppermute(last, axis, up)
        after = lax.ppermute(initial, axis, down)
        value = jnp.concatenate([before, value, after], axis=dim)
    return value


def thermal_distribution(quantity_lines):
    return jnp.minimum(quantity_lines, 0.0) + jnp.maximum(quantity_lines - LATENT_HEAT, 0.0)


def advance(current, mobility, drive, column_pad):
    solid_row = jnp.ones_like(current[:, :1, :])
    liquid_row = jnp.zeros_like(current[:, :1, :])
    row_pad = jnp.concatenate([solid_row, current, liquid_row], axis=1)
    diffusion_operator = (
        row_pad[:, :-2]
        + row_pad[:, 2:]
        + column_pad[:, :, :-2]
        + column_pad[:, :, 2:]
        - 4.0 * current
    )
    reaction = current * (1.0 - current) * (current - 0.5 - DRIVE_GAIN * drive)
    return current + DT_PHASE * mobility * (diffusion_operator + reaction)


def general(specific_heat_content, phase, mobility, positions, counts, neighbours):
    thermal_lines = thermal_distribution(specific_heat_content)
    lengthwise_margin = extended(thermal_lines, (("axial", 0),), 1, False)
    angular_margin = extended(thermal_lines, (("azim", 1),), 1, True)
    spoke_margin = jnp.pad(thermal_lines, ((0, 0), (0, 0), (1, 1)))
    diffusion_operator = (
        lengthwise_margin[2:]
        + lengthwise_margin[:-2]
        + angular_margin[:, 2:]
        + angular_margin[:, :-2]
        + spoke_margin[:, :, 2:]
        + spoke_margin[:, :, :-2]
        - 6.0 * thermal_lines
    )
    warmed_snapshot = specific_heat_content + DT_MACRO * diffusion_operator
    chilled_snapshot = thermal_distribution(warmed_snapshot)
    cells_x, cells_y, cells_z = specific_heat_content.shape
    local_x = positions[:, 0] - lax.axis_index("axial") * cells_x
    local_y = positions[:, 1] - lax.axis_index("azim") * cells_y
    inside = (local_x >= 0) & (local_x < cells_x) & (local_y >= 0) & (local_y < cells_y)
    flat_index = (
        jnp.clip(local_x, 0, cells_x - 1) * (cells_y * cells_z)
        + jnp.clip(local_y, 0, cells_y - 1) * cells_z
        + positions[:, 2]
    )
    sampled = jnp.where(inside, chilled_snapshot.reshape(-1)[flat_index], 0.0)
    patch_temps = lax.psum_scatter(sampled, ("axial", "azim"), scatter_dimension=0, tiled=True)
    capacity = phase.shape[0]
    live_slots = jnp.arange(capacity, dtype=jnp.int32) < counts[0]
    azim_count = lax.axis_size("azim")
    prev_rows = neighbours[:, 0] // capacity // azim_count * capacity + neighbours[:, 0] % capacity
    next_rows = neighbours[:, 1] // capacity // azim_count * capacity + neighbours[:, 1] % capacity
    drive = patch_temps[:, None, None]
    current = phase
    for iteration in range(PHASE_STEPS):
        edges = jnp.stack([current[:, :, 0], current[:, :, -1]], axis=1)
        gathered = lax.all_gather(edges, "axial", axis=0, tiled=True)
        left_edge = gathered[prev_rows, 1]
        right_edge = gathered[next_rows, 0]
        column_pad = jnp.concatenate(
            [left_edge[:, :, None], current, right_edge[:, :, None]], axis=2
        )
        current = advance(current, mobility, drive, column_pad)
    latent = jnp.where(live_slots, COUPLING * jnp.mean(current - phase, axis=(1, 2)), 0.0)
    phase_out = jnp.where(live_slots[:, None, None], current, phase)
    all_latent = lax.all_gather(latent, ("axial", "azim"), axis=0, tiled=True)
    released = jnp.where(inside, all_latent, 0.0)
    enthalpy_out = (
        warmed_snapshot.reshape(-1)
        .at[flat_index]
        .add(released)
        .reshape(specific_heat_content.shape)
    )
    return (enthalpy_out, phase_out)


def local_cell(x, y, a, b):
    return x - a * CX, ((y - b * CY + 1) & (NB * CY - 1)) - 1


def rank_hits(pos_ref, posb, a, b):
    for c in range(2):
        for r in range(8):
            posb[c, r : r + 1, :] = pos_ref[c : c + 1, r * 128 : r * 128 + 128]
    lx, ly = local_cell(posb[0], posb[1], a, b)
    inx = (lx >= 0) & (lx < CX)
    iny = (ly >= 0) & (ly < CY)
    touched = (inx & (ly <= CY)) | (iny & (lx >= -1) & (lx <= CX))
    mark = jnp.where(touched, 1.0, 0.0).astype(F32)
    row = lax.broadcasted_iota(I32, (128, 128), 0)
    col = lax.broadcasted_iota(I32, (128, 128), 1)
    before = jnp.where(row < col, 1.0, 0.0).astype(F32)
    within = jnp.dot(mark, before, preferred_element_type=F32)
    totals = jnp.dot(mark, jnp.ones((128, 128), F32), preferred_element_type=F32)
    row8 = lax.broadcasted_iota(I32, (8, 8), 0)
    col8 = lax.broadcasted_iota(I32, (8, 8), 1)
    above = jnp.dot(jnp.where(col8 < row8, 1.0, 0.0).astype(F32), totals, preferred_element_type=F32)
    rank = jnp.where(touched, within + above, -1.0)
    return rank, jnp.sum(touched.astype(I32))


def share_of(s, valid, spos_ref, e_ref, a, b, lane_z):
    px, py = local_cell(spos_ref[0, s], spos_ref[1, s], a, b)
    z = spos_ref[2, s]
    okx = (px >= 0) & (px < CX) & valid
    oky = (py >= 0) & (py < CY) & valid
    x0 = jnp.clip(px, 0, CX - 1)
    y0 = jnp.clip(py, 0, CY - 1)

    def part(x, y, ok):
        x, y = jnp.clip(x, 0, CX - 1), jnp.clip(y, 0, CY - 1)
        t = thermal_distribution(e_ref[x, pl.ds(y, 1), :])
        return jnp.where(ok, t, 0.0)

    own = jnp.where(okx & oky, e_ref[x0, pl.ds(y0, 1), :], 0.0)
    t = thermal_distribution(own)
    ring = (
        part(px - 1, y0, oky & (px >= 1) & (px <= CX))
        + part(px + 1, y0, oky & (px >= -1) & (px < CX - 1))
        + part(x0, py - 1, okx & (py >= 1) & (py <= CY))
        + part(x0, py + 1, okx & (py >= -1) & (py < CY - 1))
    )
    beside = (lane_z == z - 1) | (lane_z == z + 1)
    line = jnp.where(lane_z == z, own + DT_MACRO * (ring - 6.0 * t), 0.0) + jnp.where(beside, DT_MACRO * t, 0.0)
    return (line[:, 0:128] + line[:, 128:256]) + (line[:, 256:384] + line[:, 384:512])


def seam_tables(nb_ref, place_ref, recv_ref, a):
    halos = range(2 * SLOTS)
    names = [nb_ref[e % 2, e // 2] for e in halos]
    source = [n // (SLOTS * NB) for n in names]
    slot = [n % SLOTS for n in names]
    over = jnp.int32(0)
    for e in halos:
        rank = jnp.int32(0)
        for f in range(e):
            rank = rank + (source[f] == source[e]).astype(I32)
        hop = (a - source[e] + NA) % NA
        far = (hop > 0).astype(I32)
        over = jnp.maximum(over, far * (rank >= CAP).astype(I32))
        recv_ref[e] = jnp.where(hop > 0, (hop - 1) * CAP + jnp.minimum(rank, CAP - 1), 0)
        place_ref[3 * e] = source[e] * SLOTS + slot[e]
        place_ref[3 * e + 1] = 2 * slot[e] + 1 - e % 2
        place_ref[3 * e + 2] = far
    key = [2 * slot[f] + 1 - f % 2 for f in halos]
    lane = lax.broadcasted_iota(I32, (1, 128), 1)
    sends = jnp.zeros((1, 128), I32)
    for f in halos:
        turn = jnp.int32(0)
        for g in halos:
            if g != f:
                turn = turn + ((source[g] == source[f]) & (key[g] < key[f])).astype(I32)
        hop = (source[f] - a + NA) % NA
        goal = jnp.where((hop > 0) & (turn < CAP), (hop - 1) * CAP + turn, -1)
        sends = sends + jnp.where(lane == goal, f, 0)
    return sends, over


def along_rows(halves, lane):
    even, odd = halves
    axis = even.ndim - 1
    above = jnp.where(lane == 0, 1.0, pltpu.roll(odd, 1, axis))
    below = jnp.where(lane == LANES - 1, 0.0, pltpu.roll(even, LANES - 1, axis))
    return above + odd, even + below


def along_columns(c):
    n = c.shape[0]
    first = pltpu.roll(c[n - 1], 1, 0)[None]
    last = pltpu.roll(c[0], 7, 0)[None]
    return jnp.concatenate([first, c[: n - 1]], axis=0) + jnp.concatenate([c[1:], last], axis=0)


def phase_step(halves, rates, k1, k4, lane):
    beside = along_rows(halves, lane)
    out = []
    for h in range(2):
        c = halves[h]
        out.append(c + rates[h] * ((beside[h] + along_columns(c)) + c * (c * (k1 - c) - k4)))
    return tuple(out)


def main_kernel(
    pos_ref, spos_ref, nb_ref, count_ref, e_hbm, phase_hbm, mob_hbm,
    heated_ref, out_ref, latent_ref, over_ref, hits_ref,
    send_v, send_ref, recv_ref, place_ref, posb, shares,
    e_ref, t_ref, p_ref, m_ref, pt, mt, ct, eb, sb, rb, stp, stm,
    hx, hy, ty, c_out, c1, c2, sum1, lat, l1, l2, latsum, nb_t, weave, rows_v,
    load_sem, s1s, s1r, s2s, s2r, es, er, hxs, hxr, hys, hyr, l1s, l1r, l2s, l2r,
):
    a, b = lax.axis_index("axial"), lax.axis_index("azim")
    ax = [(lax.rem(a + i, NA), b) for i in range(1, NA)]
    az = [(a, lax.rem(b + i, NB)) for i in range(1, NB)]
    barrier = pltpu.get_barrier_semaphore()
    hops = [min(i // 4, 4 - i // 4) + min(i % 4, 4 - i % 4) for i in range(1, NA)]
    far_first = sorted(range(NA - 1), key=lambda k: -hops[k])
    for peer in [ax[k] for k in far_first] + az:
        pl.semaphore_signal(barrier, inc=1, device_id=peer, device_id_type=MESH)

    load_e = pltpu.make_async_copy(e_hbm, e_ref, load_sem.at[4])
    load_e.start()
    loads = []
    for k, (src, dst) in enumerate(((phase_hbm, p_ref), (mob_hbm, m_ref))):
        for tile in range(2):
            columns = pl.ds(tile * LANES, LANES)
            loads.append(pltpu.make_async_copy(src.at[:, :, columns], dst.at[:, tile], load_sem.at[2 * k + tile]))
    for load in loads:
        load.start()

    lanes1 = lax.broadcasted_iota(I32, (1, 128), 1)
    alive_all = ((lanes1 // SLOTS == a) & (lanes1 % SLOTS < count_ref[0])).astype(F32)
    sends, over = seam_tables(nb_ref, place_ref, recv_ref, a)
    send_v[...] = sends
    to_smem = pltpu.make_async_copy(send_v, send_ref, load_sem.at[5])
    to_smem.start()
    rank, count = rank_hits(pos_ref, posb, a, b)
    over = jnp.maximum(over, (count > HIT_CAP).astype(I32))
    hits_ref[0] = jnp.minimum(count, HIT_CAP)
    linear = lax.broadcasted_iota(I32, (NB, 128), 0) * 128 + lax.broadcasted_iota(I32, (NB, 128), 1)
    lane_z = lax.broadcasted_iota(I32, (1, CZ), 1)

    @pl.loop(0, HIT_CAP // HIT_GROUP)
    def _(i):
        for j in range(HIT_GROUP):
            h = i * HIT_GROUP + j
            s = jnp.sum(jnp.where(rank == h.astype(F32), linear, 0))
            hits_ref[h + 1] = jnp.clip(s, 0, NA * NB * SLOTS - 1)

    load_e.wait()

    @pl.loop(0, HIT_CAP // HIT_GROUP)
    def _(i):
        for j in range(HIT_GROUP):
            h = i * HIT_GROUP + j
            s = jnp.clip(hits_ref[h + 1], 0, NA * NB * SLOTS - 1)
            rows_v[pl.ds(h, 1), :] = share_of(s, h < count, spos_ref, e_ref, a, b, lane_z)

    values = jnp.sum(rows_v[...], axis=1, keepdims=True)
    acc = jnp.zeros((NB, 128), F32)
    for h in range(HIT_CAP):
        s = hits_ref[h + 1]
        goal = ((s // SLOTS) % NB) * 128 + (s // (SLOTS * NB)) * SLOTS + s % SLOTS
        acc = acc + jnp.where(linear == goal, values[h : h + 1], 0.0)
    shares[...] = acc

    c_out[0:NB, :] = shares[...]
    c_out[NB : NB + 1, :] = jnp.full((1, 128), over, I32).astype(F32)

    pl.semaphore_wait(barrier, len(az) + len(ax))

    for i, peer in ((k, ax[k]) for k in far_first):
        pltpu.make_async_remote_copy(c_out, c1.at[a], s1s, s1r, device_id=peer, device_id_type=MESH).start()
    c1[a] = c_out[...]

    for load in loads:
        load.wait()
    to_smem.wait()

    @pl.loop(0, SLOTS)
    def _(s):
        for h in range(2):
            for tile in range(2):
                rows = pl.ds(h, LANES, stride=2)
                ph = p_ref[s, tile, rows, :].T
                mh = m_ref[s, tile, rows, :].T * DT_PHASE
                for i in range(4):
                    place = pl.ds(tile * 4 + i, 32, stride=8)
                    pt[s, h, place, :] = ph[i * 32 : i * 32 + 32]
                    mt[s, h, place, :] = mh[i * 32 : i * 32 + 32]
                e = 2 * s + tile
                base = h * 11
                if tile == 0:
                    eb[e, base : base + 6] = ph[0:6]
                    eb[e, base + 6 : base + 11] = mh[0:5]
                    stp[s, tile, h, 0:2] = jnp.zeros((2, 128), F32)
                    stp[s, tile, h, 8:24] = ph[0:16]
                    stm[s, tile, h, 0:3] = jnp.zeros((3, 128), F32)
                    stm[s, tile, h, 8:24] = mh[0:16]
                else:
                    eb[e, base : base + 6] = ph[122:128]
                    eb[e, base + 6 : base + 11] = mh[123:128]
                    stp[s, tile, h, 0:16] = ph[112:128]
                    stp[s, tile, h, 22:24] = jnp.zeros((2, 128), F32)
                    stm[s, tile, h, 0:16] = mh[112:128]
                    stm[s, tile, h, 21:24] = jnp.zeros((3, 128), F32)

    for i, peer in ((k, ax[k]) for k in far_first):
        for n in range(i * CAP, (i + 1) * CAP):
            sb[n] = eb[jnp.clip(send_ref[0, n], 0, 2 * SLOTS - 1)]
        pltpu.make_async_remote_copy(
            sb.at[pl.ds(i * CAP, CAP)], rb.at[pl.ds(i * CAP, CAP)], es, er, device_id=peer, device_id_type=MESH
        ).start()

    @pl.loop(0, CX)
    def _(x):
        t = thermal_distribution(e_ref[x])
        t_ref[x] = t
        ty[0, x] = t[0:1]
        ty[1, x] = t[CY - 1 : CY]

    up_b, down_b = (a, lax.rem(b + 1, NB)), (a, lax.rem(b + NB - 1, NB))
    up_a, down_a = (lax.rem(a + 1, NA), b), (lax.rem(a + NA - 1, NA), b)
    y_up = pltpu.make_async_remote_copy(ty.at[1], hy.at[0], hys.at[0], hyr.at[0], device_id=up_b, device_id_type=MESH)
    y_down = pltpu.make_async_remote_copy(ty.at[0], hy.at[1], hys.at[1], hyr.at[1], device_id=down_b, device_id_type=MESH)
    y_up.start()
    y_down.start()

    whole1 = pltpu.make_async_remote_copy(
        c1.at[pl.ds(0, NA - 1)], c1.at[pl.ds(0, NA - 1)], s1s, s1r, device_id=ax[0], device_id_type=MESH
    )
    whole1.wait_recv()
    partial = jnp.sum(c1[...], axis=0)
    for j in range(NB):
        sum1[j, 0:1, :] = partial[j : j + 1]
        sum1[j, 1:2, :] = partial[NB : NB + 1]
    for i, peer in enumerate(az):
        pltpu.make_async_remote_copy(
            sum1.at[peer[1]], c2.at[b], s2s, s2r, device_id=peer, device_id_type=MESH
        ).start()
    c2[b] = sum1[b]

    x_up = pltpu.make_async_remote_copy(
        t_ref.at[CX - 1], hx.at[0], hxs.at[0], hxr.at[0], device_id=up_a, device_id_type=MESH
    )
    x_down = pltpu.make_async_remote_copy(
        t_ref.at[0], hx.at[1], hxs.at[1], hxr.at[1], device_id=down_a, device_id_type=MESH
    )
    x_up.start()
    x_down.start()

    y_up.wait()
    y_down.wait()

    line = lax.broadcasted_iota(I32, (CY, CZ), 0)
    radial = lax.broadcasted_iota(I32, (CY, CZ), 1)

    def plane(x, below, above):
        t = t_ref[x]
        ym = jnp.where(line == 0, hy[0, x], pltpu.roll(t, 1, 0))
        yp = jnp.where(line == CY - 1, hy[1, x], pltpu.roll(t, CY - 1, 0))
        zm = jnp.where(radial == 0, 0.0, pltpu.roll(t, 1, 1))
        zp = jnp.where(radial == CZ - 1, 0.0, pltpu.roll(t, CZ - 1, 1))
        heated_ref[x] = e_ref[x] + DT_MACRO * ((below + above) + (ym + yp) + (zm + zp) - 6.0 * t)

    @pl.loop(1, CX - 1)
    def _(x):
        plane(x, t_ref[x - 1], t_ref[x + 1])

    whole2 = pltpu.make_async_remote_copy(
        c2.at[pl.ds(0, NB - 1)], c2.at[pl.ds(0, NB - 1)], s2s, s2r, device_id=az[0], device_id_type=MESH
    )
    whole2.wait_recv()
    total = jnp.sum(c2[...], axis=0)
    over_ref[...] = total[1:2]
    temps = thermal_distribution(total[0:1])

    def temp_of(index):
        return jnp.sum(jnp.where(lanes1 == index, temps, 0.0), axis=1, keepdims=True)

    cells = (SIDE // 8, 8, LANES)
    lane_full = lax.broadcasted_iota(I32, cells, 2)
    column = lax.broadcasted_iota(I32, cells, 1) * (SIDE // 8) + lax.broadcasted_iota(I32, cells, 0)
    body = (column >= 6) & (column < SIDE - 6)

    @pl.loop(0, SLOTS)
    def _(s):
        tau = temp_of(a * SLOTS + s)
        nb_t[s] = jnp.broadcast_to(tau, (1, 128))
        k1, k4 = 1.5 + DRIVE_GAIN * tau, 4.5 + DRIVE_GAIN * tau
        start = (pt[s, 0].reshape(cells), pt[s, 1].reshape(cells))
        rates = (mt[s, 0].reshape(cells), mt[s, 1].reshape(cells))
        cur = start
        for _step in range(PHASE_STEPS):
            cur = phase_step(cur, rates, k1, k4, lane_full)
        ct[s, 0] = cur[0].reshape(SIDE, LANES)
        ct[s, 1] = cur[1].reshape(SIDE, LANES)
        change = (cur[0] - start[0]) + (cur[1] - start[1])
        latsum[s] = jnp.sum(jnp.sum(jnp.where(body, change, 0.0), axis=0), axis=0, keepdims=True)

    whole_e = pltpu.make_async_remote_copy(sb, rb, es, er, device_id=ax[0], device_id_type=MESH)
    whole_e.wait_recv()

    @pl.loop(0, SLOTS)
    def _(s):
        for side in range(2):
            e = 2 * s + side
            near = eb[place_ref[3 * e + 1]]
            far = rb[recv_ref[e]]
            is_far = jnp.broadcast_to(place_ref[3 * e + 2], (EDGE_ROWS, 128)) > 0
            edge = jnp.where(is_far, far, near)
            for h in range(2):
                first = 2 if side == 0 else 16
                stp[s, side, h, first : first + 6] = edge[h * 11 : h * 11 + 6]
                first = 3 if side == 0 else 16
                stm[s, side, h, first : first + 5] = edge[h * 11 + 6 : h * 11 + 11]
            nb_t[SLOTS + e] = jnp.broadcast_to(temp_of(place_ref[3 * e]), (1, 128))

    strip = (3, 8, LANES)
    lane_strip = lax.broadcasted_iota(I32, strip, 2)
    row_strip = lax.broadcasted_iota(I32, strip, 1) * 3 + lax.broadcasted_iota(I32, strip, 0)
    lat[...] = jnp.zeros((1, 128), F32)

    def woven(ref, s, side, h):
        return jnp.stack([ref[s, side, h, pl.ds(j, 8, stride=3), :] for j in range(3)], axis=0)

    @pl.loop(0, SLOTS // STRIP_GROUP)
    def _(n):
        pairs = [(n * STRIP_GROUP + k, side) for k in range(STRIP_GROUP) for side in range(2)]
        curs, rates, ks = [], [], []
        for s, side in pairs:
            curs.append((woven(stp, s, side, 0), woven(stp, s, side, 1)))
            rates.append((woven(stm, s, side, 0), woven(stm, s, side, 1)))
            outer = row_strip < 8 if side == 0 else row_strip >= 16
            ks.append(DRIVE_GAIN * jnp.where(outer, nb_t[SLOTS + 2 * s + side][None], nb_t[s][None]))
        starts = curs
        for _step in range(PHASE_STEPS):
            curs = [phase_step(c, r, 1.5 + k, 4.5 + k, lane_strip) for c, r, k in zip(curs, rates, ks)]
        for k in range(STRIP_GROUP):
            s = n * STRIP_GROUP + k
            total_s = latsum[s]
            for side in range(2):
                q = 2 * k + side
                low = 8 if side == 0 else 10
                for h in range(2):
                    for j in range(3):
                        stp[s, side, h, pl.ds(j, 8, stride=3), :] = curs[q][h][j]
                    if side == 0:
                        ct[s, h, pl.ds(0, 6, stride=8), :] = stp[s, side, h, low : low + 6]
                    else:
                        ct[s, h, pl.ds(26 * 8 + 7, 6, stride=8), :] = stp[s, side, h, low : low + 6]
                kept = (row_strip >= low) & (row_strip < low + 6)
                change = (curs[q][0] - starts[q][0]) + (curs[q][1] - starts[q][1])
                total_s = total_s + jnp.sum(jnp.sum(jnp.where(kept, change, 0.0), axis=0), axis=0, keepdims=True)
            value = jnp.sum(total_s, axis=1, keepdims=True) * (COUPLING / (SIDE * SIDE))
            lat[...] = jnp.where(lanes1 == a * SLOTS + s, jnp.where(alive_all > 0.5, value, 0.0), lat[...])

    for i, peer in ((k, ax[k]) for k in far_first):
        pltpu.make_async_remote_copy(lat, l1.at[a], l1s, l1r, device_id=peer, device_id_type=MESH).start()
    l1[a] = lat[...]

    x_up.wait()
    x_down.wait()
    plane(0, jnp.where(a > 0, 1.0, 0.0).astype(F32) * hx[0], t_ref[1])
    plane(CX - 1, t_ref[CX - 2], jnp.where(a < NA - 1, 1.0, 0.0).astype(F32) * hx[1])

    whole_l1 = pltpu.make_async_remote_copy(
        l1.at[pl.ds(0, NA - 1)], l1.at[pl.ds(0, NA - 1)], l1s, l1r, device_id=ax[0], device_id_type=MESH
    )
    whole_l1.wait_recv()
    column = jnp.sum(l1[...], axis=0)
    l2[b] = column
    for i, peer in enumerate(az):
        pltpu.make_async_remote_copy(l2.at[b], l2.at[b], l2s, l2r, device_id=peer, device_id_type=MESH).start()

    @pl.loop(0, SLOTS)
    def _(s):
        alive = jnp.sum(jnp.where(lanes1 == a * SLOTS + s, alive_all, 0.0), axis=1, keepdims=True)
        for h in range(2):
            for tile in range(2):
                parts = []
                for i in range(4):
                    place = pl.ds(tile * 4 + i, 32, stride=8)
                    parts.append(jnp.where(alive > 0.5, ct[s, h, place, :], pt[s, h, place, :]))
                weave[tile, pl.ds(h, LANES, stride=2), :] = jnp.concatenate(parts, axis=0).T
        for tile in range(2):
            out_ref[s, :, tile * LANES : tile * LANES + LANES] = weave[tile]

    whole_l2 = pltpu.make_async_remote_copy(
        l2.at[pl.ds(0, NB - 1)], l2.at[pl.ds(0, NB - 1)], l2s, l2r, device_id=az[0], device_id_type=MESH
    )
    whole_l2.wait_recv()
    for j in range(NB):
        latent_ref[j : j + 1, :] = l2[j]

    whole1.wait_send()
    whole2.wait_send()
    whole_e.wait_send()
    whole_l1.wait_send()
    whole_l2.wait_send()


def release_kernel(hits_ref, spos_ref, lat_ref, heated_hbm, phase_hbm, out_hbm, phase_out_hbm, grid_ref, sem):
    move = pltpu.make_async_copy(phase_hbm, phase_out_hbm, sem.at[0])
    move.start()
    load = pltpu.make_async_copy(heated_hbm, grid_ref, sem.at[1])
    load.start()
    a, b = lax.axis_index("axial"), lax.axis_index("azim")
    lane = lax.broadcasted_iota(I32, (1, CZ), 1)
    load.wait()

    def add(h, carry):
        s = hits_ref[h + 1]
        px, py = local_cell(spos_ref[0, s], spos_ref[1, s], a, b)
        z = spos_ref[2, s]
        inside = (px >= 0) & (px < CX) & (py >= 0) & (py < CY)
        x0 = jnp.clip(px, 0, CX - 1)
        y0 = jnp.clip(py, 0, CY - 1)
        lat = lat_ref[((s // SLOTS) % NB) * 128 + (s // (SLOTS * NB)) * SLOTS + s % SLOTS]
        value = jnp.where(inside, lat, 0.0)
        grid_ref[x0, pl.ds(y0, 1), :] = grid_ref[x0, pl.ds(y0, 1), :] + jnp.where(lane == z, value, 0.0)
        return carry

    lax.fori_loop(0, hits_ref[0], add, 0)
    store = pltpu.make_async_copy(grid_ref, out_hbm, sem.at[2])
    store.start()
    store.wait()
    move.wait()


def spec(space):
    return pl.BlockSpec(memory_space=space)


def shards(specific_heat_content, phase, mobility, positions, counts, neighbours):
    pos = positions.T
    near = neighbours.T

    heated, phase_new, latents, over_all, hits = pl.pallas_call(
        main_kernel,
        out_shape=(
            jax.ShapeDtypeStruct((CX, CY, CZ), F32),
            jax.ShapeDtypeStruct((SLOTS, SIDE, SIDE), F32),
            jax.ShapeDtypeStruct((NB, 128), F32),
            jax.ShapeDtypeStruct((1, 128), F32),
            jax.ShapeDtypeStruct((HIT_CAP + 8,), I32),
        ),
        in_specs=[spec(VMEM)] + [spec(SMEM)] * 3 + [spec(pl.ANY)] * 3,
        out_specs=(spec(VMEM), spec(VMEM), spec(VMEM), spec(VMEM), spec(SMEM)),
        scratch_shapes=[
            VMEM((1, 128), I32),
            SMEM((1, 128), I32),
            SMEM((2 * SLOTS,), I32),
            SMEM((6 * SLOTS,), I32),
            VMEM((2, NB, 128), I32),
            VMEM((NB, 128), F32),
            VMEM((CX, CY, CZ), F32),
            VMEM((CX, CY, CZ), F32),
            VMEM((SLOTS, 2, SIDE, LANES), F32),
            VMEM((SLOTS, 2, SIDE, LANES), F32),
            VMEM((SLOTS, 2, SIDE, 128), F32),
            VMEM((SLOTS, 2, SIDE, 128), F32),
            VMEM((SLOTS, 2, SIDE, 128), F32),
            VMEM((2 * SLOTS, EDGE_ROWS, 128), F32),
            VMEM(((NA - 1) * CAP, EDGE_ROWS, 128), F32),
            VMEM(((NA - 1) * CAP, EDGE_ROWS, 128), F32),
            VMEM((SLOTS, 2, 2, 24, 128), F32),
            VMEM((SLOTS, 2, 2, 24, 128), F32),
            VMEM((2, CY, CZ), F32),
            VMEM((2, CX, 1, CZ), F32),
            VMEM((2, CX, 1, CZ), F32),
            VMEM((NB + 1, 128), F32),
            VMEM((NA, NB + 1, 128), F32),
            VMEM((NB, 2, 128), F32),
            VMEM((NB, 2, 128), F32),
            VMEM((1, 128), F32),
            VMEM((NA, 1, 128), F32),
            VMEM((NB, 1, 128), F32),
            VMEM((SLOTS, 1, 128), F32),
            VMEM((3 * SLOTS, 1, 128), F32),
            VMEM((2, SIDE, LANES), F32),
            VMEM((HIT_CAP, LANES), F32),
            DMA((6,)),
            DMA, DMA, DMA, DMA, DMA, DMA,
            DMA((2,)), DMA((2,)), DMA((2,)), DMA((2,)),
            DMA, DMA, DMA, DMA,
        ],
        compiler_params=pltpu.CompilerParams(
            collective_id=0, has_side_effects=True, vmem_limit_bytes=48 << 20
        ),
        name="couple",
    )(pos, pos, near, counts, specific_heat_content, phase, mobility)

    def finish():
        return pl.pallas_call(
            release_kernel,
            out_shape=(
                jax.ShapeDtypeStruct((CX, CY, CZ), F32),
                jax.ShapeDtypeStruct((SLOTS, SIDE, SIDE), F32),
            ),
            in_specs=[spec(SMEM)] * 3 + [spec(pl.ANY)] * 2,
            out_specs=(spec(pl.ANY), spec(pl.ANY)),
            scratch_shapes=[VMEM((CX, CY, CZ), F32), DMA((3,))],
            compiler_params=pltpu.CompilerParams(vmem_limit_bytes=16 << 20),
            name="release",
        )(hits, pos, latents.reshape(-1), heated, phase_new)

    def whole():
        return general(specific_heat_content, phase, mobility, positions, counts, neighbours)

    return lax.cond(over_all[0, 0] > 0.5, whole, finish)


def solution(mesh):
    in_specs = (
        P("axial", "azim", None),
        P(("axial", "azim"), None, None),
        P(("axial", "azim"), None, None),
        P(),
        P(("axial", "azim")),
        P(("axial", "azim"), None),
    )
    out_specs = (P("axial", "azim", None), P(("axial", "azim"), None, None))
    return jax.shard_map(shards, mesh=mesh, in_specs=in_specs, out_specs=out_specs, check_vma=False)
```
